32 devices in a mesh: edge: 8 (over z, y), rep: 4 (over x, core).
Axes of the slice: x: 2, y: 2, z: 4, core: 2. Of those that a mesh axis runs over, the one named last changes fastest.
Arguments:
- atom_features: bfloat16 [4, 8192, 256], P('rep', 'edge'), may hold values from -6 to 6
- distances: float32 [4, 131072], P('rep', 'edge'), may hold values from 0.5 to 6
- source_index: int32 [4, 131072], P('rep', 'edge'), may hold values from 0 to 1023
- slot_index: int32 [4, 8192, 16], P('rep', 'edge'), may hold values from 0 to 16383, as said below
- live_mask: int32 [4, 8192, 16], P('rep', 'edge'), may hold values from 0 to 1, as said below
- output_cot: bfloat16 [4, 8192, 256], P('rep', 'edge'), may hold values from -6 to 6
- energy_cot: float32 [4, 8192], P('rep', 'edge'), may hold values from -6 to 6
- attention_weight: float32 [256, 768], P(None, 'edge'), may hold values from -0.375 to 0.375
- attention_first: float32 [256, 768], P(None, 'edge'), may hold values from -320 to 320
- attention_second: float32 [256, 768], P(None, 'edge'), may hold values from 2949.12 to 11796.48
- output_weight: float32 [256, 256], P(None, 'edge'), may hold values from -1.5 to 1.5
- output_first: float32 [256, 256], P(None, 'edge'), may hold values from -512 to 512
- output_second: float32 [256, 256], P(None, 'edge'), may hold values from 8192 to 32768
- gateup_weight: float32 [256, 2048], P(None, 'edge'), may hold values from -0.375 to 0.375
- gateup_first: float32 [256, 2048], P(None, 'edge'), may hold values from -448 to 448
- gateup_second: float32 [256, 2048], P(None, 'edge'), may hold values from 5242.88 to 20971.52
- down_weight: float32 [1024, 256], P(None, 'edge'), may hold values from -0.1875 to 0.1875
- down_first: float32 [1024, 256], P(None, 'edge'), may hold values from -896 to 896
- down_second: float32 [1024, 256], P(None, 'edge'), may hold values from 20971.52 to 83886.08
- basis_weight: float32 [600, 512], P(None, 'edge'), may hold values from -3 to 3
- basis_first: float32 [600, 512], P(None, 'edge'), may hold values from -224 to 224
- basis_second: float32 [600, 512], P(None, 'edge'), may hold values from 1310.72 to 5242.88
- readout_weight: float32 [256], P('edge'), may hold values from -0.375 to 0.375
- readout_first: float32 [256], P('edge'), may hold values from -1536 to 1536
- readout_second: float32 [256], P('edge'), may hold values from 73728 to 294912
- norm_gains: float32 [2, 256], P(None, 'edge'), may hold values from 0.5 to 1.5
- gains_first: float32 [2, 256], P(None, 'edge'), may hold values from -1024 to 1024
- gains_second: float32 [2, 256], P(None, 'edge'), may hold values from 32768 to 131072
Outputs:
- block_out: bfloat16 [4, 8192, 256], P('rep', 'edge')
- energy: float32 [4, 8192], P('rep', 'edge')
- input_grad: float32 [4, 8192, 256], P('rep', 'edge')
- attention_first_new: float32 [256, 768], P(None, 'edge')
- attention_second_new: float32 [256, 768], P(None, 'edge')
- attention_weight_new: float32 [256, 768], P(None, 'edge')
- output_first_new: float32 [256, 256], P(None, 'edge')
- output_second_new: float32 [256, 256], P(None, 'edge')
- output_weight_new: float32 [256, 256], P(None, 'edge')
- gateup_first_new: float32 [256, 2048], P(None, 'edge')
- gateup_second_new: float32 [256, 2048], P(None, 'edge')
- gateup_weight_new: float32 [256, 2048], P(None, 'edge')
- down_first_new: float32 [1024, 256], P(None, 'edge')
- down_second_new: float32 [1024, 256], P(None, 'edge')
- down_weight_new: float32 [1024, 256], P(None, 'edge')
- basis_first_new: float32 [600, 512], P(None, 'edge')
- basis_second_new: float32 [600, 512], P(None, 'edge')
- basis_weight_new: float32 [600, 512], P(None, 'edge')
- readout_first_new: float32 [256], P('edge')
- readout_second_new: float32 [256], P('edge')
- readout_weight_new: float32 [256], P('edge')
- gains_first_new: float32 [2, 256], P(None, 'edge')
- gains_second_new: float32 [2, 256], P(None, 'edge')
- norm_gains_new: float32 [2, 256], P(None, 'edge')
- attention_low: bfloat16 [256, 768], P(None, 'edge')
- output_low: bfloat16 [256, 256], P(None, 'edge')
- gateup_low: bfloat16 [256, 2048], P(None, 'edge')
- down_low: bfloat16 [1024, 256], P(None, 'edge')
- basis_low: bfloat16 [600, 512], P(None, 'edge')
The draws below stay inside these ranges and needn't reach their ends.
Inputs may be any that keep to these rules, and one draw needn't show every extreme that they name: `slot_index`: for each graph batch and each owner's 1024 atoms, the 16384 entries form a permutation of 0 to 16383, so every edge row is named by exactly one slot. `live_mask`: each atom's live slots come first, and its first slot is live.
All inputs are finite; a program needn't handle non-finite values.
Results may differ from the reference program's by a relative error of at most 0.017.
Values may be sent and summed in bfloat16 or wider, within the bound.
No kernel may reach another device: no remote copies, remote signals or barrier semaphores. Data moves between devices by JAX's collectives and lax.ppermute only.
A program may use at most 320 MiB of HBM per device.

```python
import math
import jax
import jax.numpy as jnp
from jax import lax

H = 256
HEADS = 8
FF = 1024
NB = 600
A_DEV = 1024
K = 16
STEP = 5
HEAD_DIM = 32
E_DEV = 16384
SLOT = 2048
ATOMS = 8192
EDGES = 131072
REPS = 4
TOKENS = 32768


def draw_slot_index(key, part):
    key = jax.random.fold_in(key, 11)
    owners = ATOMS // A_DEV
    many_keys = jax.random.split(key, REPS * owners)
    orders = jax.vmap(lambda single: jax.random.permutation(single, E_DEV))(many_keys)
    return orders.reshape(REPS, ATOMS, K).astype(jnp.int32)


def draw_live_mask(key, part):
    key = jax.random.fold_in(key, 23)
    counts = jax.random.randint(key, (REPS, ATOMS, 1), 1, K + 1)
    return (jnp.arange(K, dtype=jnp.int32)[None, None, :] < counts).astype(jnp.int32)


def touch_ends(values, stream_key, low, top_value):
    longest = values.shape.index(max(values.shape))
    spots = []
    for shift in (0, 1):
        where = [jax.random.randint(jax.random.fold_in(stream_key, axis), (), 0, length) for axis, length in enumerate(values.shape)]
        where[longest] = (where[longest] + shift) % values.shape[longest]
        spots.append(tuple(where))
    return values.at[spots[0]].set(low).at[spots[1]].set(top_value)


def levels(own_key, extent, pieces, least, high):
    def one(axis_at, shards_of):
        heights = jax.random.uniform(jax.random.fold_in(jax.random.fold_in(own_key, 6), axis_at), (shards_of,), jnp.float32, least / len(pieces), high / len(pieces))
        return jnp.repeat(jnp.exp(heights), extent[axis_at] // shards_of).reshape((-1,) + (1,) * (len(extent) - axis_at - 1))

    gain = one(*pieces[0])
    for cut in pieces[1:]:
        gain = gain * one(*cut)
    return gain


def gaussian(stream_key, extent, deviation, most, cuts=(), kind=jnp.bfloat16):
    drawn = jax.random.normal(stream_key, extent, jnp.float32) * deviation
    if len(cuts) > 0:
        drawn = levels(stream_key, extent, cuts, -0.22, 0.18) * drawn
    return jnp.clip(drawn, min=-most, max=most).astype(kind)


def setup_inputs(seed: int = 0) -> dict:
    key_list = jax.random.split(jax.random.key(seed), 29)
    return {
        "atom_features": gaussian(key_list[0], (REPS, ATOMS, H), 1.0, 6.0, ((0, 4), (1, 8))),
        "distances": jnp.clip(0.5 + 5.5 * jax.random.uniform(key_list[1], (REPS, EDGES), jnp.float32) ** levels(key_list[1], (REPS, EDGES), ((0, 4), (1, 8)), -0.2, 0.2), 0.5, 6.0),
        "source_index": touch_ends(jax.random.randint(key_list[2], (REPS, EDGES), 0, A_DEV), jax.random.fold_in(key_list[2], 1), 0, A_DEV - 1).astype(jnp.int32),
        "slot_index": draw_slot_index(jax.random.fold_in(key_list[28], 71), 0),
        "live_mask": draw_live_mask(jax.random.fold_in(key_list[28], 71), 0),
        "output_cot": gaussian(key_list[5], (REPS, ATOMS, H), 1.0, 6.0, ((0, 4), (1, 8))),
        "energy_cot": gaussian(key_list[6], (REPS, ATOMS), 1.0, 6.0, ((0, 4), (1, 8)), jnp.float32),
        "attention_weight": gaussian(key_list[7], (H, 3 * H), H ** -0.5, 0.375, ((1, 8),), jnp.float32),
        "attention_first": gaussian(key_list[8], (H, 3 * H), (0.3 * TOKENS ** 0.5), 320.0, ((1, 8),), jnp.float32),
        "attention_second": jnp.clip(jnp.exp(math.log(11796.48) - 1.3862944 * jax.random.uniform(key_list[9], (H, 3 * H), jnp.float32) ** levels(key_list[9], (H, 3 * H), ((1, 8),), -0.2, 0.2)), 2949.12, 11796.48),
        "output_weight": gaussian(key_list[10], (H, H), (H // 16) ** -0.5, 1.5, ((1, 8),), jnp.float32),
        "output_first": gaussian(key_list[11], (H, H), (0.5 * TOKENS ** 0.5), 512.0, ((1, 8),), jnp.float32),
        "output_second": jnp.clip(jnp.exp(math.log(32768.0) - 1.3862944 * jax.random.uniform(key_list[12], (H, H), jnp.float32) ** levels(key_list[12], (H, H), ((1, 8),), -0.2, 0.2)), 8192.0, 32768.0),
        "gateup_weight": gaussian(key_list[13], (H, 2 * FF), H ** -0.5, 0.375, ((1, 8),), jnp.float32),
        "gateup_first": gaussian(key_list[14], (H, 2 * FF), (0.4 * TOKENS ** 0.5), 448.0, ((1, 8),), jnp.float32),
        "gateup_second": jnp.clip(jnp.exp(math.log(20971.52) - 1.3862944 * jax.random.uniform(key_list[15], (H, 2 * FF), jnp.float32) ** levels(key_list[15], (H, 2 * FF), ((1, 8),), -0.2, 0.2)), 5242.88, 20971.52),
        "down_weight": gaussian(key_list[16], (FF, H), FF ** -0.5, 0.1875, ((1, 8),), jnp.float32),
        "down_first": gaussian(key_list[17], (FF, H), (0.8 * TOKENS ** 0.5), 896.0, ((1, 8),), jnp.float32),
        "down_second": jnp.clip(jnp.exp(math.log(83886.08) - 1.3862944 * jax.random.uniform(key_list[18], (FF, H), jnp.float32) ** levels(key_list[18], (FF, H), ((1, 8),), -0.2, 0.2)), 20971.52, 83886.08),
        "basis_weight": gaussian(key_list[19], (NB, 2 * H), 4 ** -0.5, 3.0, ((1, 8),), jnp.float32),
        "basis_first": gaussian(key_list[20], (NB, 2 * H), (0.2 * TOKENS ** 0.5), 224.0, ((1, 8),), jnp.float32),
        "basis_second": jnp.clip(jnp.exp(math.log(5242.88) - 1.3862944 * jax.random.uniform(key_list[21], (NB, 2 * H), jnp.float32) ** levels(key_list[21], (NB, 2 * H), ((1, 8),), -0.2, 0.2)), 1310.72, 5242.88),
        "readout_weight": gaussian(key_list[22], (H,), H ** -0.5, 0.375, ((0, 8),), jnp.float32),
        "readout_first": gaussian(key_list[23], (H,), (1.5 * TOKENS ** 0.5), 1536.0, ((0, 8),), jnp.float32),
        "readout_second": jnp.clip(jnp.exp(math.log(294912.0) - 1.3862944 * jax.random.uniform(key_list[24], (H,), jnp.float32) ** levels(key_list[24], (H,), ((0, 8),), -0.2, 0.2)), 73728.0, 294912.0),
        "norm_gains": jnp.clip(1.0 + 0.1 * jax.random.normal(key_list[25], (2, H), jnp.float32), 0.5, 1.5),
        "gains_first": gaussian(key_list[26], (2, H), (1.0 * TOKENS ** 0.5), 1024.0, ((1, 8),), jnp.float32),
        "gains_second": jnp.clip(jnp.exp(math.log(131072.0) - 1.3862944 * jax.random.uniform(key_list[27], (2, H), jnp.float32) ** levels(key_list[27], (2, H), ((1, 8),), -0.2, 0.2)), 32768.0, 131072.0),
    }


EPS = 1e-06
CUTOFF = 6.0
BETA_ONE = 0.5
BETA_TWO = 0.5
ADAM_EPS = 1e-08
DECAY = 0.01

@jax.custom_vjp
def low(v):
    return lax.optimization_barrier(v.astype(jnp.bfloat16)).astype(jnp.float32)

@jax.custom_vjp
def low_back(v):
    return v

def low_keep(v):
    return (low(v), None)

def low_pass(kept, grad):
    return (grad,)

def back_keep(v):
    return (v, None)

def back_low(kept, grad):
    return (low(grad),)
low.defvjp(low_keep, low_pass)
low_back.defvjp(back_keep, back_low)

def product(left, right):
    return jnp.dot(left, right, precision=lax.Precision.HIGHEST, preferred_element_type=jnp.float32)

def radial_basis(edge_len):
    centres = jnp.arange(NB).astype(jnp.float32) * (CUTOFF / (NB - 1))
    spread = 2.0 * CUTOFF / (NB - 1)
    return jnp.exp(-jnp.square((edge_len[:, None] - centres) / spread))

def adamw_step(weight, first_mom, second, gradient, step_rate):
    first_new = BETA_ONE * first_mom + (1.0 - BETA_ONE) * gradient
    second_new = BETA_TWO * second + (1.0 - BETA_TWO) * gradient * gradient
    fix_one = 1.0 - BETA_ONE ** STEP
    fix_two = 1.0 - BETA_TWO ** STEP
    direction = first_new / fix_one / (jnp.sqrt(second_new / fix_two) + ADAM_EPS) + DECAY * weight
    return (first_new, second_new, weight - step_rate * direction)

def reference(atom_features, distances, source_index, slot_index, live_mask, output_cot, energy_cot, attention_weight, attention_first, attention_second, output_weight, output_first, output_second, gateup_weight, gateup_first, gateup_second, down_weight, down_first, down_second, basis_weight, basis_first, basis_second, readout_weight, readout_first, readout_second, norm_gains, gains_first, gains_second):
    masters = (attention_weight, output_weight, gateup_weight, down_weight, basis_weight, readout_weight, norm_gains)

    def forward(weights, features):
        lowered = tuple((low(weight) for weight in weights))
        proj_attention, proj_output, proj_gateup, proj_down, proj_basis, reader, gain_pair = lowered
        scaling = HEAD_DIM ** (-0.5)

        def replica(items):
            feature, edge_len, sources, slot_ids, is_live = items
            inv_one = lax.rsqrt(lax.optimization_barrier(jnp.mean(feature * feature, axis=-1, keepdims=True)) + EPS)
            normed_one = low(feature * inv_one * gain_pair[0])
            query_vals = low_back(product(normed_one, proj_attention[:, :H]))
            queries = low(query_vals).reshape(ATOMS, HEADS, HEAD_DIM)
            owner_edge = jnp.arange(EDGES, dtype=jnp.int32) // E_DEV
            global_src = sources + owner_edge * A_DEV
            edge_rows = low_back(normed_one[global_src])
            radial = low(radial_basis(edge_len))
            edge_kv = low(low_back(product(edge_rows, proj_attention[:, H:]) + product(radial, proj_basis)))
            owner_atom = (jnp.arange(ATOMS, dtype=jnp.int32) // A_DEV)[:, None]
            edge_ids = slot_ids // SLOT * E_DEV + owner_atom * SLOT + slot_ids % SLOT
            paired = edge_kv[edge_ids]
            key_rows = paired[..., :H].reshape(ATOMS, K, HEADS, HEAD_DIM)
            values = paired[..., H:].reshape(ATOMS, K, HEADS, HEAD_DIM)
            scores = low_back(jnp.einsum('ahd,akhd->akh', queries, key_rows, precision=lax.Precision.HIGHEST) * scaling)
            masked = jnp.where(is_live[..., None] > 0, scores, -1e+30)
            row_top = lax.optimization_barrier(jnp.max(masked, axis=1, keepdims=True))
            exp_terms = jnp.exp(masked - row_top)
            softmax = low(exp_terms / lax.optimization_barrier(jnp.sum(exp_terms, axis=1, keepdims=True)))
            mixture = low(low_back(jnp.einsum('akh,akhd->ahd', softmax, values, precision=lax.Precision.HIGHEST)))
            after_attn = feature + low_back(product(mixture.reshape(ATOMS, H), proj_output))
            inv_two = lax.rsqrt(lax.optimization_barrier(jnp.mean(after_attn * after_attn, axis=-1, keepdims=True)) + EPS)
            normed_two = low(after_attn * inv_two * gain_pair[1])
            gate_up = low_back(product(normed_two, proj_gateup))
            hidden = low(jax.nn.silu(gate_up[:, :FF]) * gate_up[:, FF:])
            result = after_attn + low_back(product(hidden, proj_down))
            return (result, lax.optimization_barrier(jnp.sum(result * reader, axis=-1)))
        return lax.map(jax.checkpoint(replica), (features, distances, source_index, slot_index, live_mask))
    features = atom_features.astype(jnp.float32)
    (result, energy), pullback = jax.vjp(forward, masters, features)
    gradients, input_grad = pullback((output_cot.astype(jnp.float32), energy_cot))
    step_rates = (H ** (-0.5), (H // 16) ** (-0.5), H ** (-0.5), FF ** (-0.5), 0.5, H ** (-0.5), 0.2)
    firsts = (attention_first, output_first, gateup_first, down_first, basis_first, readout_first, gains_first)
    seconds = (attention_second, output_second, gateup_second, down_second, basis_second, readout_second, gains_second)
    updated = [adamw_step(masters[number], firsts[number], seconds[number], gradients[number], step_rates[number]) for number in range(7)]
    return (result.astype(jnp.bfloat16), energy, input_grad, updated[0][0], updated[0][1], updated[0][2], updated[1][0], updated[1][1], updated[1][2], updated[2][0], updated[2][1], updated[2][2], updated[3][0], updated[3][1], updated[3][2], updated[4][0], updated[4][1], updated[4][2], updated[5][0], updated[5][1], updated[5][2], updated[6][0], updated[6][1], updated[6][2], updated[0][2].astype(jnp.bfloat16), updated[1][2].astype(jnp.bfloat16), updated[2][2].astype(jnp.bfloat16), updated[3][2].astype(jnp.bfloat16), updated[4][2].astype(jnp.bfloat16))
```

```python
import functools
import math

import jax
import jax.numpy as jnp
import numpy as np
from jax import lax
from jax.experimental import pallas as pl
from jax.experimental.pallas import tpu as pltpu
from jax.sharding import PartitionSpec as P

H = 256
HEADS = 8
FF = 1024
NB = 600
STEP = 5
HEAD_DIM = 32

EPS = 1e-06
CUTOFF = 6.0
BETA_ONE = 0.5
BETA_TWO = 0.5
ADAM_EPS = 1e-08
DECAY = 0.01

LANES = 128
NB_PAD = 640
NB_ROWS = 768
WIDE = H + NB_PAD
CHUNK = 1024
BLOCK = 128
GROUP = 1024
UNROLL = 16
VMEM_BYTES = 60 * 1024 * 1024

F32 = jnp.float32
BF16 = jnp.bfloat16


def dot_nn(left, right):
    return jnp.dot(left, right, preferred_element_type=F32)


def dot_nt(left, right):
    return lax.dot_general(left, right, (((1,), (1,)), ((), ())), preferred_element_type=F32)


def dot_tn(left, right):
    return lax.dot_general(left, right, (((0,), (0,)), ((), ())), preferred_element_type=F32)


def inverse_rms(rows):
    return lax.rsqrt(jnp.mean(rows * rows, axis=-1, keepdims=True) + EPS)


def edges_forward(order_ref, mine_ref, other_ref, small_ref, dist_ref, src_ref, *rest):
    kept_ref, normed_ref = rest[-2:]
    atoms = mine_ref.shape[0]

    def norm(ref):
        features = ref[...].astype(F32)
        normed_ref[...] = (features * inverse_rms(features) * small_ref[0:1, :]).astype(BF16)

    first = pl.program_id(1) == 0
    pl.when(jnp.logical_and(first, pl.program_id(0) == 0))(lambda: norm(mine_ref))
    pl.when(jnp.logical_and(first, pl.program_id(0) == 1))(lambda: norm(other_ref))
    atom_lane = lax.broadcasted_iota(jnp.int32, (1, atoms), 1).astype(F32)
    centres = lax.broadcasted_iota(jnp.int32, (1, NB_PAD), 1).astype(F32) * (CUTOFF / (NB - 1))
    per_spread = math.sqrt(math.log2(math.e)) / (2.0 * CUTOFF / (NB - 1))
    picks, bases = [], []
    for column in range(dist_ref.shape[3]):
        source = src_ref[0, 0, :, column : column + 1]
        picks.append(jnp.where(source == atom_lane, 1.0, 0.0).astype(BF16))
        offset = (dist_ref[0, 0, :, column : column + 1] - centres) * per_spread
        bases.append(jnp.exp2(-(offset * offset)).astype(BF16))
    kept_ref[:, :H] = dot_nn(jnp.concatenate(picks, axis=0), normed_ref[...]).astype(BF16)
    kept_ref[:, H:] = jnp.concatenate(bases, axis=0)


def atoms_kernel(
    ins, blocks, outs, owners,
    idx_ref, core_ref, kept_ref, x_ref, cot_ref, ecot_ref, count_ref, small_ref,
    wide_ref, query_ref, output_ref, gateup_ref, down_ref,
    block_ref, energy_ref, after_ref, dnorm_ref, drows_ref, mine_ref, theirs_ref,
    rows, stage, products, spread_out, sum_up,
    gwide_ref, ggateup_ref, gdown_ref, goutput_ref, gquery_ref, gsmall_ref,
):
    step = pl.program_id(0)
    scaling = HEAD_DIM ** (-0.5)
    slots = stage.shape[0] // (4 * BLOCK)
    pairs = slots * HEADS

    @pl.when(step == 0)
    def _():
        for ref in (gwide_ref, ggateup_ref, gdown_ref, goutput_ref, gquery_ref, gsmall_ref):
            ref[...] = jnp.zeros_like(ref)
        lane = lax.broadcasted_iota(jnp.int32, (pairs, slots * H), 1) // HEAD_DIM
        pair = lax.broadcasted_iota(jnp.int32, (pairs, slots * H), 0)
        spread_out[...] = jnp.where(lane == pair, 1.0, 0.0).astype(BF16)
        lane = lax.broadcasted_iota(jnp.int32, (slots * H, pairs), 0) // HEAD_DIM
        pair = lax.broadcasted_iota(jnp.int32, (slots * H, pairs), 1)
        sum_up[...] = jnp.where(lane == pair, 1.0, 0.0).astype(BF16)

    @pl.when(step < ins)
    def _():
        base = pl.multiple_of(step * (CHUNK * 4), CHUNK * 4)
        edge_kv = dot_nt(kept_ref[...], wide_ref[...]).astype(BF16).astype(F32)
        for part in range(4):
            rows[pl.ds(base + part, CHUNK, stride=4), :] = edge_kv[
                :, part * LANES : (part + 1) * LANES
            ]

    @pl.when(jnp.logical_and(step >= ins, step < ins + blocks))
    def _():
        block = step - ins
        total = slots * BLOCK
        base = block * total

        def fetch(turn, carry):
            for inner in range(UNROLL):
                row = turn * UNROLL + inner
                at = pl.multiple_of(idx_ref[base + row], 4)
                stage[pl.ds(pl.multiple_of(row * 4, 4), 4), :] = rows[pl.ds(at, 4), :]
            return carry

        lax.fori_loop(0, total // UNROLL, fetch, 0)

        def staged(slot, part):
            first = slot * (4 * BLOCK) + 2 * part
            return jnp.concatenate(
                [stage[pl.ds(first + half, BLOCK, stride=4), :] for half in (0, 1)], axis=1
            )

        def put(slot, part, value):
            first = slot * (4 * BLOCK) + 2 * part
            for half in (0, 1):
                stage[pl.ds(first + half, BLOCK, stride=4), :] = value[
                    :, half * LANES : (half + 1) * LANES
                ]

        def over_slots(values, combine):
            shift = HEADS
            while shift < pairs:
                values = combine(values, pltpu.roll(values, shift, 1))
                shift *= 2
            return values

        def over_features(left, part):
            for slot in range(slots):
                products[:, slot * H : (slot + 1) * H] = (left * staged(slot, part)).astype(BF16)
            return dot_nn(products[...], sum_up[...])

        gain_one = small_ref[0:1, :]
        gain_two = small_ref[1:2, :]
        reader = small_ref[2:3, :]
        features = x_ref[...].astype(F32)
        inv_one = inverse_rms(features)
        normed_one = (features * inv_one * gain_one).astype(BF16)
        queries = dot_nt(normed_one, query_ref[...]).astype(BF16).astype(F32)

        scores = over_features(queries, 0) * scaling
        slot_of = lax.broadcasted_iota(jnp.int32, (1, pairs), 1) // HEADS
        scores = jnp.where(slot_of.astype(F32) < count_ref[...], scores, -1e30)
        terms = jnp.exp(scores - over_slots(scores, jnp.maximum))
        soft = terms / over_slots(terms, jnp.add)
        soft_low = soft.astype(BF16)

        def spread(values, slot):
            return dot_nn(values, spread_out[:, slot * H : (slot + 1) * H])

        mixture = jnp.zeros((BLOCK, H), F32)
        for slot in range(slots):
            mixture += spread(soft_low, slot) * staged(slot, 1)
        mixture = mixture.astype(BF16)

        after = features + dot_nt(mixture, output_ref[...])
        inv_two = inverse_rms(after)
        normed_two = (after * inv_two * gain_two).astype(BF16)
        gate_up = dot_nt(normed_two, gateup_ref[...])
        ff = gate_up.shape[1] // 2
        gate, up_part = gate_up[:, :ff], gate_up[:, ff:]
        gate_sig = 1.0 / (1.0 + jnp.exp(-gate))
        swished = gate * gate_sig
        hidden = (swished * up_part).astype(BF16)
        result = after + dot_nt(hidden, down_ref[...])
        block_ref[...] = result.astype(BF16)
        energy_ref[...] = jnp.broadcast_to(
            jnp.sum(result * reader, axis=-1, keepdims=True), energy_ref.shape
        )
        energy_row = ecot_ref[...]
        d_result = cot_ref[...].astype(F32) + energy_row * reader
        grad_read = jnp.sum(energy_row * result, axis=0, keepdims=True)
        d_ffn = d_result.astype(BF16)
        gdown_ref[...] += dot_tn(d_ffn, hidden)
        d_hidden = dot_nn(d_ffn, down_ref[...])
        d_gate = d_hidden * up_part * gate_sig * (1.0 + gate * (1.0 - gate_sig))
        d_gate_up = jnp.concatenate(
            [d_gate.astype(BF16), (d_hidden * swished).astype(BF16)], axis=1
        )
        ggateup_ref[...] += dot_tn(d_gate_up, normed_two)
        d_normed_two = dot_nn(d_gate_up, gateup_ref[...])
        scaled = d_normed_two * gain_two
        grad_gain_two = jnp.sum(d_normed_two * after * inv_two, axis=0, keepdims=True)
        d_after = (
            d_result
            + inv_two * scaled
            - after * (inv_two * inv_two * inv_two)
            * jnp.mean(scaled * after, axis=-1, keepdims=True)
        )
        after_ref[...] = d_after
        d_attn = d_after.astype(BF16)
        goutput_ref[...] += dot_tn(d_attn, mixture)
        d_mixture = dot_nn(d_attn, output_ref[...]).astype(BF16).astype(F32)

        d_soft = over_features(d_mixture, 1)
        d_scores = soft * (d_soft - over_slots(soft * d_soft, jnp.add))
        d_scores = d_scores.astype(BF16)
        scaled_queries = queries * scaling
        d_queries = jnp.zeros((BLOCK, H), F32)
        for slot in range(slots):
            wide_scores = spread(d_scores, slot)
            d_queries += wide_scores * staged(slot, 0)
            put(slot, 0, wide_scores * scaled_queries)
            put(slot, 1, spread(soft_low, slot) * d_mixture)
        d_queries = (d_queries * scaling).astype(BF16)
        gquery_ref[...] += dot_tn(d_queries, normed_one)
        d_normed = dot_nn(d_queries, query_ref[...])
        dnorm_ref[...] = d_normed
        grad_gain_one = jnp.sum(d_normed * features * inv_one, axis=0, keepdims=True)
        gsmall_ref[0:1, :] += grad_gain_one
        gsmall_ref[1:2, :] += grad_gain_two
        gsmall_ref[2:3, :] += grad_read

        def spill(turn, carry):
            for inner in range(UNROLL):
                row = turn * UNROLL + inner
                at = pl.multiple_of(idx_ref[base + row], 4)
                rows[pl.ds(at, 4), :] = stage[pl.ds(pl.multiple_of(row * 4, 4), 4), :]
            return carry

        lax.fori_loop(0, total // UNROLL, spill, 0)

    @pl.when(step >= ins + blocks)
    def _():
        base = pl.multiple_of((step - ins - blocks) * (CHUNK * 4), CHUNK * 4)
        d_edges = jnp.concatenate(
            [rows[pl.ds(base + part, CHUNK, stride=4), :].astype(BF16) for part in range(4)], axis=1
        )
        gwide_ref[...] += dot_tn(d_edges, kept_ref[...])
        drows_ref[...] = dot_nn(d_edges, wide_ref[:, :H]).astype(BF16)

    @pl.when(step == ins + blocks + outs - 1)
    def _():
        shares = gwide_ref[:, :H] * wide_ref[:, :H].astype(F32)
        gsmall_ref[0:1, :] += jnp.sum(shares, axis=0, keepdims=True) / small_ref[0:1, :]
        size = mine_ref.shape[0]
        height = size // owners
        for owner in range(owners):
            for half in (0, 1):
                at = half * size + owner * height
                for ref, first, count, columns in packed_pieces(
                    owner, owners, gquery_ref, gwide_ref, ggateup_ref, gdown_ref, goutput_ref
                ):
                    for low in range(columns.start + half * LANES, columns.stop, H):
                        if low < ref.shape[1]:
                            rows[at : at + count, :] = ref[
                                first : first + count, low : low + LANES
                            ]
                        at += count
                rows[at : at + 8, :] = gsmall_ref[:, half * LANES : (half + 1) * LANES]
        core = core_ref[0]
        for ref, half in ((mine_ref, core), (theirs_ref, 1 - core)):
            ref[...] = rows[pl.ds(pl.multiple_of(half * size, 8), size), :].astype(BF16)


def packed_pieces(owner, owners, query, wide, gateup, down, output):
    count = 3 * H // owners
    first, last = owner * count, (owner + 1) * count
    if first < H:
        yield query, first, min(last, H) - first, range(H)
    if last > H:
        yield wide, max(first, H) - H, last - max(first, H), range(H)
    share = 2 * H // owners
    yield wide, owner * share, share, range(H, H + NB_ROWS)
    for ref in (gateup, down, output):
        share = ref.shape[0] // owners
        yield ref, owner * share, share, range(ref.shape[1])


def edges_backward(order_ref, rows_ref, src_ref, mine_ref, other_ref):
    d_rows = rows_ref[...]
    source = src_ref[0]
    step = 256

    def sums(ref):
        for start in range(0, ref.shape[0], step):
            atom = lax.broadcasted_iota(jnp.int32, (step, 1), 0).astype(F32) + float(start)
            pick = jnp.where(atom == source, 1.0, 0.0).astype(BF16)
            ref[start : start + step, :] = dot_nn(pick, d_rows).astype(ref.dtype)

    pl.when(pl.program_id(0) == 0)(lambda: sums(mine_ref))
    pl.when(pl.program_id(0) == 1)(lambda: sums(other_ref))


def adamw_step(weight, first_mom, second, gradient, step_rate):
    first_new = BETA_ONE * first_mom + (1.0 - BETA_ONE) * gradient
    second_new = BETA_TWO * second + (1.0 - BETA_TWO) * gradient * gradient
    fix_one = 1.0 - BETA_ONE**STEP
    fix_two = 1.0 - BETA_TWO**STEP
    direction = first_new / fix_one / (jnp.sqrt(second_new / fix_two) + ADAM_EPS) + DECAY * weight
    return (first_new, second_new, weight - step_rate * direction)


def whole_spec(shape):
    return pl.BlockSpec(shape, lambda *_: (0,) * len(shape), pipeline_mode=pl.Buffered(1))


def run_edges_forward(turn, order, mine, other, small, dist_cols, src_cols, before):
    atoms = mine.shape[0]
    owners, groups, _, columns = dist_cols.shape
    size = columns * LANES
    edges = owners * groups * size

    def picked(i, g, order_ref):
        return (order_ref[2 * turn + i], g, 0, 0)

    def written(i, g, order_ref):
        return ((2 * turn + i) * groups + g, 0)

    return pl.pallas_call(
        edges_forward,
        grid_spec=pltpu.PrefetchScalarGridSpec(
            num_scalar_prefetch=1,
            grid=(2, groups),
            in_specs=[
                whole_spec(mine.shape),
                whole_spec(other.shape),
                whole_spec(small.shape),
                pl.BlockSpec((1, 1, LANES, columns), picked),
                pl.BlockSpec((1, 1, LANES, columns), picked),
            ]
            + [pl.BlockSpec(memory_space=pl.ANY)] * len(before),
            out_specs=pl.BlockSpec((size, WIDE), written),
            scratch_shapes=[pltpu.VMEM((atoms, H), BF16)],
        ),
        out_shape=jax.ShapeDtypeStruct((edges, WIDE), BF16),
        input_output_aliases={6: 0} if before else {},
        compiler_params=pltpu.CompilerParams(vmem_limit_bytes=VMEM_BYTES),
        cost_estimate=pl.CostEstimate(
            flops=4 * groups * size * atoms * H,
            bytes_accessed=2 * groups * size * 2 * WIDE + 2 * atoms * H * 2,
            transcendentals=2 * groups * size * NB_PAD,
        ),
    )(order, mine, other, small, dist_cols, src_cols, *before)


def run_atoms(
    owners, idx, core, kept, features, cot, ecot, count, small, wide, query, output, gateup, down
):
    edges, atoms = kept.shape[0], features.shape[0]
    ins, blocks = edges // CHUNK, atoms // BLOCK
    outs = ins
    slots = edges // atoms
    ff = down.shape[1]
    height = (3 * H + 3 * 2 * H + gateup.shape[0] + ff // H * H + H) // owners + 8

    def atom_block(i):
        return (jnp.clip(i - ins, 0, blocks - 1), 0)

    def edge_block(i):
        return (jnp.where(i < ins, i, jnp.maximum(i - ins - blocks, 0)), 0)

    return pl.pallas_call(
        functools.partial(atoms_kernel, ins, blocks, outs, owners),
        grid=(ins + blocks + outs,),
        in_specs=[
            pl.BlockSpec(memory_space=pltpu.SMEM),
            pl.BlockSpec(memory_space=pltpu.SMEM),
            pl.BlockSpec((CHUNK, WIDE), edge_block),
            pl.BlockSpec((BLOCK, H), atom_block),
            pl.BlockSpec((BLOCK, H), atom_block),
            pl.BlockSpec((BLOCK, 1), atom_block),
            pl.BlockSpec((BLOCK, 1), atom_block),
            whole_spec(small.shape),
            whole_spec(wide.shape),
            whole_spec(query.shape),
            whole_spec(output.shape),
            whole_spec(gateup.shape),
            whole_spec(down.shape),
        ],
        out_specs=[
            pl.BlockSpec((BLOCK, H), atom_block),
            pl.BlockSpec((BLOCK, LANES), atom_block),
            pl.BlockSpec((BLOCK, H), atom_block),
            pl.BlockSpec((BLOCK, H), atom_block),
            pl.BlockSpec((CHUNK, H), lambda i: (jnp.maximum(i - ins - blocks, 0), 0)),
            whole_spec((owners * height, LANES)),
            whole_spec((owners * height, LANES)),
        ],
        out_shape=[
            jax.ShapeDtypeStruct((atoms, H), BF16),
            jax.ShapeDtypeStruct((atoms, LANES), F32),
            jax.ShapeDtypeStruct((atoms, H), F32),
            jax.ShapeDtypeStruct((atoms, H), F32),
            jax.ShapeDtypeStruct((edges, H), BF16),
            jax.ShapeDtypeStruct((owners * height, LANES), BF16),
            jax.ShapeDtypeStruct((owners * height, LANES), BF16),
        ],
        scratch_shapes=[
            pltpu.VMEM((edges * 4 + 8, LANES), F32),
            pltpu.VMEM((slots * BLOCK * 4 + 8, LANES), F32),
            pltpu.VMEM((BLOCK, slots * H), BF16),
            pltpu.VMEM((slots * HEADS, slots * H), BF16),
            pltpu.VMEM((slots * H, slots * HEADS), BF16),
            pltpu.VMEM(wide.shape, F32),
            pltpu.VMEM(gateup.shape, F32),
            pltpu.VMEM(down.shape, F32),
            pltpu.VMEM(output.shape, F32),
            pltpu.VMEM(query.shape, F32),
            pltpu.VMEM((8, H), F32),
        ],
        compiler_params=pltpu.CompilerParams(vmem_limit_bytes=VMEM_BYTES),
        cost_estimate=pl.CostEstimate(
            flops=2 * edges * H * (WIDE * 4 + H * 8) + 2 * atoms * H * ff * 9,
            bytes_accessed=edges * WIDE * 4 + edges * H * 2 + ff * H * 3 * 6,
            transcendentals=edges * HEADS,
        ),
    )(idx, core, kept, features, cot, ecot, count, small, wide, query, output, gateup, down)


def run_edges_backward(turn, order, d_rows, src_rows, atoms):
    owners, sent = src_rows.shape[0], src_rows.shape[2]
    return pl.pallas_call(
        edges_backward,
        grid_spec=pltpu.PrefetchScalarGridSpec(
            num_scalar_prefetch=1,
            grid=(2,),
            in_specs=[
                pl.BlockSpec((sent, H), lambda i, order_ref: (2 * turn + i, 0)),
                pl.BlockSpec((1, 1, sent), lambda i, order_ref: (order_ref[2 * turn + i], 0, 0)),
            ],
            out_specs=[whole_spec((atoms, H)), whole_spec((atoms, H))],
        ),
        out_shape=[jax.ShapeDtypeStruct((atoms, H), BF16)] * 2,
        compiler_params=pltpu.CompilerParams(vmem_limit_bytes=VMEM_BYTES),
        cost_estimate=pl.CostEstimate(
            flops=4 * sent * atoms * H,
            bytes_accessed=2 * sent * 2 * H + 4 * atoms * H,
            transcendentals=0,
        ),
    )(order, d_rows, src_rows)


def halves(axis_size):
    return range((axis_size - 1).bit_length())


def across(array, bit):
    size = lax.axis_size("rep")
    return lax.ppermute(array, "rep", [(r, r ^ (1 << bit)) for r in range(size)])


def gather_rows(rows):
    owners, reps = lax.axis_size("edge"), lax.axis_size("rep")
    me = lax.axis_index("rep")
    share = rows.shape[0] // reps
    part = lax.dynamic_slice_in_dim(rows, me * share, share, 0)
    held = lax.all_to_all(
        jnp.broadcast_to(part[None], (owners, share, H)), "edge", 0, 0, tiled=True
    )
    for bit in reversed(halves(reps)):
        fetched = across(held, bit)
        upper = (me >> bit) & 1 == 1
        held = jnp.stack([jnp.where(upper, fetched, held), jnp.where(upper, held, fetched)])
    bits = len(halves(reps))
    held = held.transpose((bits,) + tuple(reversed(range(bits))) + (bits + 1, bits + 2))
    return held.reshape(owners, reps * share, H)


def reduce_rows(mine, theirs):
    owners, reps = lax.axis_size("edge"), lax.axis_size("rep")
    me = lax.axis_index("rep")
    totals = mine.astype(F32) + across(theirs, 0).astype(F32)
    totals = totals.reshape(owners, -1, LANES)
    for bit in halves(reps)[1:]:
        half = totals.shape[1] // 2
        upper = (me >> bit) & 1
        sent = lax.dynamic_slice_in_dim(totals, (1 - upper) * half, half, 1)
        kept = lax.dynamic_slice_in_dim(totals, upper * half, half, 1)
        totals = kept + across(sent.astype(BF16), bit).astype(F32)
    pieces = lax.all_to_all(totals.astype(BF16), "edge", 0, 0, tiled=True)
    held = jnp.sum(pieces.astype(F32), axis=0)
    for bit in reversed(halves(reps)):
        fetched = across(held, bit)
        upper = (me >> bit) & 1 == 1
        held = jnp.concatenate(
            [jnp.where(upper, fetched, held), jnp.where(upper, held, fetched)],
            axis=0 if bit > 0 else 1,
        )
    return held


def ring_of(owners):
    pairs = owners // 2
    return [*range(0, pairs, 2), *reversed(range(1, pairs, 2))]


def ring_step(array):
    owners = lax.axis_size("edge")
    ring = ring_of(owners)
    moves = [
        (2 * here + side, 2 * ring[(at + 1) % len(ring)] + side)
        for at, here in enumerate(ring)
        for side in (0, 1)
    ]
    return lax.ppermute(array, "edge", moves)


def pair_swap(array):
    owners = lax.axis_size("edge")
    return lax.ppermute(array, "edge", [(e, e ^ 1) for e in range(owners)])


def arrival_order(owners):
    ring = ring_of(owners)
    table = np.zeros((owners, owners), np.int32)
    for at, here in enumerate(ring):
        for side in (0, 1):
            for turn in range(len(ring)):
                source = 2 * ring[at - turn]
                table[2 * here + side, 2 * turn : 2 * turn + 2] = (source + side, source + 1 - side)
    return table


def pad_rows(array, multiple):
    short = -array.shape[0] % multiple
    return jnp.pad(array, ((0, short), (0, 0)))


def unstack(pieces, rows, width):
    return pieces.reshape(width // H, rows, H).transpose(1, 0, 2).reshape(rows, width)


def local(
    atom_features,
    distances,
    source_index,
    slot_index,
    live_mask,
    output_cot,
    energy_cot,
    attention_weight,
    attention_first,
    attention_second,
    output_weight,
    output_first,
    output_second,
    gateup_weight,
    gateup_first,
    gateup_second,
    down_weight,
    down_first,
    down_second,
    basis_weight,
    basis_first,
    basis_second,
    readout_weight,
    readout_first,
    readout_second,
    norm_gains,
    gains_first,
    gains_second,
):
    features = atom_features[0]
    atoms = features.shape[0]
    slots = slot_index.shape[2]
    edges = atoms * slots
    owners = H // output_weight.shape[1]
    sent = edges // owners
    wa, wo, wg, wd, wb, wr = (
        attention_weight.shape[1],
        output_weight.shape[1],
        gateup_weight.shape[1],
        down_weight.shape[1],
        basis_weight.shape[1],
        readout_weight.shape[0],
    )

    dist = distances[0]
    high = lax.reduce_precision(dist, 8, 7)
    middle = lax.reduce_precision(dist - high, 8, 7)
    lower = dist - high - middle
    source = source_index[0]
    pieces = (high, middle, lower, source >> 5, source & 31)
    meta = jnp.stack([piece.astype(BF16) for piece in pieces])
    meta = meta.reshape(5, owners, sent // H, H).transpose(1, 0, 2, 3)
    meta_rows = 5 * sent // H
    thin = jnp.concatenate([norm_gains, readout_weight[None]], axis=0).astype(BF16).reshape(1, 1, -1)
    thin = jnp.broadcast_to(
        jnp.pad(thin, ((0, 0), (0, 7), (0, H - thin.shape[2]))), (owners, 8, H)
    )
    meta = jnp.concatenate([meta.reshape(owners, meta_rows, H), thin], axis=1)
    meta = lax.all_to_all(meta, "edge", 0, 0, tiled=True)
    small = meta[:, meta_rows, : 3 * wr].reshape(owners, 3, wr)
    small = small.transpose(1, 0, 2).reshape(3, H)
    small = jnp.pad(small.astype(F32), ((0, 5), (0, 0)))
    pieces = meta[:, :meta_rows].reshape(owners, 5, sent).astype(F32)
    dist = pieces[:, 0] + pieces[:, 1] + pieces[:, 2]
    source = pieces[:, 3] * 32.0 + pieces[:, 4]

    basis_rows = jnp.pad(basis_weight.T.astype(BF16), ((0, 0), (0, NB_ROWS - NB)))
    weight_rows = pad_rows(
        jnp.concatenate(
            [
                attention_weight.T.astype(BF16),
                basis_rows.reshape(3 * wb, H),
                gateup_weight.T.astype(BF16),
                down_weight.T.astype(BF16).reshape(wd * (FF // H), H),
                output_weight.T.astype(BF16),
            ],
            axis=0,
        ),
        8 * lax.axis_size("rep"),
    )
    weight_rows, meta = lax.optimization_barrier((weight_rows, meta))
    weight_rows = gather_rows(weight_rows)
    at = 0
    fulls = []
    for width, rows in ((H, wa), (NB_ROWS, wb), (H, wg), (FF, wd), (H, wo)):
        count = rows * width // H
        fulls.append(weight_rows[:, at : at + count].reshape(owners * rows, width))
        at += count
    attention_rows, basis_rows, gateup_rows, down_rows, output_rows = fulls
    query_rows, kv_rows = attention_rows[:H], attention_rows[H:]
    wide = jnp.concatenate([kv_rows, basis_rows[:, :NB_PAD]], axis=1)

    size = min(GROUP, sent)
    dist_cols, src_cols = (
        values.reshape(owners, sent // size, size // LANES, LANES).transpose(0, 1, 3, 2)
        for values in (dist, source)
    )
    src_rows = source[:, None]

    table = arrival_order(owners)
    me = lax.axis_index("edge")
    order = jnp.asarray(table)[me]
    place = jnp.asarray(np.argsort(table, axis=1).astype(np.int32))[me]
    turns = owners // 2
    mine, before = features, ()
    for turn in range(turns):
        if turn > 0:
            mine = ring_step(mine)
        before = (
            run_edges_forward(
                turn, order, mine, pair_swap(mine), small, dist_cols, src_cols, before
            ),
        )
    (kept,) = before

    slot_ids = slot_index[0]
    slot_owner = slot_ids // sent
    arrived = sum(jnp.where(slot_owner == s, place[s], 0) for s in range(owners))
    arrived = arrived * sent + slot_ids % sent
    idx = arrived.reshape(atoms // BLOCK, BLOCK, slots).transpose(0, 2, 1).reshape(-1) * 4
    count = jnp.sum(live_mask[0], axis=1, keepdims=True).astype(F32)
    core = (lax.axis_index("rep") & 1).astype(jnp.int32)[None]
    block_out, energy, d_after, d_normed_own, d_rows, grads_mine, grads_theirs = run_atoms(
        owners,
        idx,
        core,
        kept,
        features,
        output_cot[0],
        energy_cot[0][:, None],
        count,
        small,
        wide,
        query_rows,
        output_rows,
        gateup_rows,
        down_rows,
    )
    shard = reduce_rows(grads_mine, grads_theirs)

    running = None
    for turn in [*range(1, turns), 0]:
        part, part_other = run_edges_backward(turn, order, d_rows, src_rows, atoms)
        total = part.astype(F32) + pair_swap(part_other).astype(F32)
        if running is not None:
            total = total + ring_step(running).astype(F32)
        running = total.astype(BF16)
    d_from_edges = total

    features = features.astype(F32)
    inv_one = inverse_rms(features)
    d_normed_one = d_normed_own + d_from_edges
    scaled = d_normed_one * small[0:1]
    input_grad = (
        d_after
        + inv_one * scaled
        - features * inv_one**3 * jnp.mean(scaled * features, axis=-1, keepdims=True)
    )

    cuts = np.cumsum([wa, 3 * wb, wg, wd * (FF // H), wo])
    thin_shard = lax.dynamic_slice_in_dim(shard[cuts[4] : cuts[4] + 3], me * wr, wr, 1)
    gradients = (
        shard[: cuts[0]].T,
        shard[cuts[3] : cuts[4]].T,
        shard[cuts[1] : cuts[2]].T,
        unstack(shard[cuts[2] : cuts[3]], wd, FF).T,
        unstack(shard[cuts[0] : cuts[1]], wb, NB_ROWS)[:, :NB].T,
        thin_shard[2],
        thin_shard[:2],
    )
    step_rates = (
        H ** (-0.5),
        (H // 16) ** (-0.5),
        H ** (-0.5),
        FF ** (-0.5),
        0.5,
        H ** (-0.5),
        0.2,
    )
    masters = (
        attention_weight,
        output_weight,
        gateup_weight,
        down_weight,
        basis_weight,
        readout_weight,
        norm_gains,
    )
    firsts = (
        attention_first,
        output_first,
        gateup_first,
        down_first,
        basis_first,
        readout_first,
        gains_first,
    )
    seconds = (
        attention_second,
        output_second,
        gateup_second,
        down_second,
        basis_second,
        readout_second,
        gains_second,
    )
    updated = [
        adamw_step(
            masters[number], firsts[number], seconds[number], gradients[number], step_rates[number]
        )
        for number in range(7)
    ]
    flat = [array for triple in updated for array in triple]
    lows = [updated[number][2].astype(BF16) for number in range(5)]
    return (block_out[None], energy[:, 0][None], input_grad[None], *flat, *lows)


def solution(mesh):
    matrix = P(None, "edge")
    rows = P("rep", "edge", None)
    pairs = P("rep", "edge")
    weights = (matrix,) * 15 + (P("edge"),) * 3 + (matrix,) * 3
    return jax.shard_map(
        local,
        mesh=mesh,
        in_specs=(rows, pairs, pairs, rows, rows, rows, pairs) + weights,
        out_specs=(rows, pairs, rows) + weights + (matrix,) * 5,
        check_vma=False,
    )
```

```python
import functools
import math

import jax
import jax.numpy as jnp
import numpy as np
from jax import lax
from jax.experimental import pallas as pl
from jax.experimental.pallas import tpu as pltpu
from jax.sharding import PartitionSpec as P

H = 256
HEADS = 8
FF = 1024
NB = 600
STEP = 5
HEAD_DIM = 32

EPS = 1e-06
CUTOFF = 6.0
BETA_ONE = 0.5
BETA_TWO = 0.5
ADAM_EPS = 1e-08
DECAY = 0.01

LANES = 128
NB_PAD = 640
NB_ROWS = 768
WIDE = H + NB_PAD
CHUNK = 1024
BLOCK = 128
GROUP = 1024
UNROLL = 16
VMEM_BYTES = 60 * 1024 * 1024

F32 = jnp.float32
BF16 = jnp.bfloat16


def dot_nn(left, right):
    return jnp.dot(left, right, preferred_element_type=F32)


def dot_nt(left, right):
    return lax.dot_general(left, right, (((1,), (1,)), ((), ())), preferred_element_type=F32)


def dot_tn(left, right):
    return lax.dot_general(left, right, (((0,), (0,)), ((), ())), preferred_element_type=F32)


def inverse_rms(rows):
    return lax.rsqrt(jnp.mean(rows * rows, axis=-1, keepdims=True) + EPS)


def edges_forward(count, order_ref, small_ref, dist_ref, src_ref, *rest):
    feature_refs, (kept_ref, normed_ref) = rest[:count], rest[-2:]
    atoms = normed_ref.shape[0]

    def norm(ref):
        features = ref[...].astype(F32)
        normed_ref[...] = (features * inverse_rms(features) * small_ref[0:1, :]).astype(BF16)

    first = pl.program_id(1) == 0
    for number, ref in enumerate(feature_refs):
        pl.when(jnp.logical_and(first, pl.program_id(0) == number))(functools.partial(norm, ref))
    atom_lane = lax.broadcasted_iota(jnp.int32, (1, atoms), 1).astype(F32)
    centres = lax.broadcasted_iota(jnp.int32, (1, NB_PAD), 1).astype(F32) * (CUTOFF / (NB - 1))
    per_spread = math.sqrt(math.log2(math.e)) / (2.0 * CUTOFF / (NB - 1))
    picks, bases = [], []
    for column in range(dist_ref.shape[3]):
        source = src_ref[0, 0, :, column : column + 1]
        picks.append(jnp.where(source == atom_lane, 1.0, 0.0).astype(BF16))
        offset = (dist_ref[0, 0, :, column : column + 1] - centres) * per_spread
        bases.append(jnp.exp2(-(offset * offset)).astype(BF16))
    kept_ref[:, :H] = dot_nn(jnp.concatenate(picks, axis=0), normed_ref[...]).astype(BF16)
    kept_ref[:, H:] = jnp.concatenate(bases, axis=0)


def atoms_kernel(
    ins, blocks, outs, owners,
    idx_ref, core_ref, kept_ref, x_ref, cot_ref, ecot_ref, count_ref, small_ref,
    wide_ref, query_ref, output_ref, gateup_ref, down_ref,
    block_ref, energy_ref, after_ref, dnorm_ref, drows_ref, mine_ref, theirs_ref,
    rows, stage, products, spread_out, sum_up,
    gwide_ref, ggateup_ref, gdown_ref, goutput_ref, gquery_ref, gsmall_ref,
):
    step = pl.program_id(0)
    scaling = HEAD_DIM ** (-0.5)
    slots = stage.shape[0] // (4 * BLOCK)
    pairs = slots * HEADS

    @pl.when(step == 0)
    def _():
        for ref in (gwide_ref, ggateup_ref, gdown_ref, goutput_ref, gquery_ref, gsmall_ref):
            ref[...] = jnp.zeros_like(ref)
        lane = lax.broadcasted_iota(jnp.int32, (pairs, slots * H), 1) // HEAD_DIM
        pair = lax.broadcasted_iota(jnp.int32, (pairs, slots * H), 0)
        spread_out[...] = jnp.where(lane == pair, 1.0, 0.0).astype(BF16)
        lane = lax.broadcasted_iota(jnp.int32, (slots * H, pairs), 0) // HEAD_DIM
        pair = lax.broadcasted_iota(jnp.int32, (slots * H, pairs), 1)
        sum_up[...] = jnp.where(lane == pair, 1.0, 0.0).astype(BF16)

    @pl.when(step < ins)
    def _():
        base = pl.multiple_of(step * (CHUNK * 4), CHUNK * 4)
        edge_kv = dot_nt(kept_ref[...], wide_ref[...]).astype(BF16).astype(F32)
        for part in range(4):
            rows[pl.ds(base + part, CHUNK, stride=4), :] = edge_kv[
                :, part * LANES : (part + 1) * LANES
            ]

    @pl.when(jnp.logical_and(step >= ins, step < ins + blocks))
    def _():
        block = step - ins
        total = slots * BLOCK
        base = block * total

        def fetch(turn, carry):
            for inner in range(UNROLL):
                row = turn * UNROLL + inner
                at = pl.multiple_of(idx_ref[base + row], 4)
                stage[pl.ds(pl.multiple_of(row * 4, 4), 4), :] = rows[pl.ds(at, 4), :]
            return carry

        lax.fori_loop(0, total // UNROLL, fetch, 0)

        def staged(slot, part):
            first = slot * (4 * BLOCK) + 2 * part
            return jnp.concatenate(
                [stage[pl.ds(first + half, BLOCK, stride=4), :] for half in (0, 1)], axis=1
            )

        def put(slot, part, value):
            first = slot * (4 * BLOCK) + 2 * part
            for half in (0, 1):
                stage[pl.ds(first + half, BLOCK, stride=4), :] = value[
                    :, half * LANES : (half + 1) * LANES
                ]

        def over_slots(values, combine):
            shift = HEADS
            while shift < pairs:
                values = combine(values, pltpu.roll(values, shift, 1))
                shift *= 2
            return values

        def over_features(left, part):
            for slot in range(slots):
                products[:, slot * H : (slot + 1) * H] = (left * staged(slot, part)).astype(BF16)
            return dot_nn(products[...], sum_up[...])

        gain_one = small_ref[0:1, :]
        gain_two = small_ref[1:2, :]
        reader = small_ref[2:3, :]
        features = x_ref[...].astype(F32)
        inv_one = inverse_rms(features)
        normed_one = (features * inv_one * gain_one).astype(BF16)
        queries = dot_nt(normed_one, query_ref[...]).astype(BF16).astype(F32)

        scores = over_features(queries, 0) * scaling
        slot_of = lax.broadcasted_iota(jnp.int32, (1, pairs), 1) // HEADS
        scores = jnp.where(slot_of.astype(F32) < count_ref[...], scores, -1e30)
        terms = jnp.exp(scores - over_slots(scores, jnp.maximum))
        soft = terms / over_slots(terms, jnp.add)
        soft_low = soft.astype(BF16)

        def spread(values, slot):
            return dot_nn(values, spread_out[:, slot * H : (slot + 1) * H])

        mixture = jnp.zeros((BLOCK, H), F32)
        for slot in range(slots):
            mixture += spread(soft_low, slot) * staged(slot, 1)
        mixture = mixture.astype(BF16)

        after = features + dot_nt(mixture, output_ref[...])
        inv_two = inverse_rms(after)
        normed_two = (after * inv_two * gain_two).astype(BF16)
        gate_up = dot_nt(normed_two, gateup_ref[...])
        ff = gate_up.shape[1] // 2
        gate, up_part = gate_up[:, :ff], gate_up[:, ff:]
        gate_sig = 1.0 / (1.0 + jnp.exp(-gate))
        swished = gate * gate_sig
        hidden = (swished * up_part).astype(BF16)
        result = after + dot_nt(hidden, down_ref[...])
        block_ref[...] = result.astype(BF16)
        energy_ref[...] = jnp.broadcast_to(
            jnp.sum(result * reader, axis=-1, keepdims=True), energy_ref.shape
        )
        energy_row = ecot_ref[...]
        d_result = cot_ref[...].astype(F32) + energy_row * reader
        grad_read = jnp.sum(energy_row * result, axis=0, keepdims=True)
        d_ffn = d_result.astype(BF16)
        gdown_ref[...] += dot_tn(d_ffn, hidden)
        d_hidden = dot_nn(d_ffn, down_ref[...])
        d_gate = d_hidden * up_part * gate_sig * (1.0 + gate * (1.0 - gate_sig))
        d_gate_up = jnp.concatenate(
            [d_gate.astype(BF16), (d_hidden * swished).astype(BF16)], axis=1
        )
        ggateup_ref[...] += dot_tn(d_gate_up, normed_two)
        d_normed_two = dot_nn(d_gate_up, gateup_ref[...])
        scaled = d_normed_two * gain_two
        grad_gain_two = jnp.sum(d_normed_two * after * inv_two, axis=0, keepdims=True)
        d_after = (
            d_result
            + inv_two * scaled
            - after * (inv_two * inv_two * inv_two)
            * jnp.mean(scaled * after, axis=-1, keepdims=True)
        )
        after_ref[...] = d_after
        d_attn = d_after.astype(BF16)
        goutput_ref[...] += dot_tn(d_attn, mixture)
        d_mixture = dot_nn(d_attn, output_ref[...]).astype(BF16).astype(F32)

        d_soft = over_features(d_mixture, 1)
        d_scores = soft * (d_soft - over_slots(soft * d_soft, jnp.add))
        d_scores = d_scores.astype(BF16)
        scaled_queries = queries * scaling
        d_queries = jnp.zeros((BLOCK, H), F32)
        for slot in range(slots):
            wide_scores = spread(d_scores, slot)
            d_queries += wide_scores * staged(slot, 0)
            put(slot, 0, wide_scores * scaled_queries)
            put(slot, 1, spread(soft_low, slot) * d_mixture)
        d_queries = (d_queries * scaling).astype(BF16)
        gquery_ref[...] += dot_tn(d_queries, normed_one)
        d_normed = dot_nn(d_queries, query_ref[...])
        dnorm_ref[...] = d_normed
        grad_gain_one = jnp.sum(d_normed * features * inv_one, axis=0, keepdims=True)
        gsmall_ref[0:1, :] += grad_gain_one
        gsmall_ref[1:2, :] += grad_gain_two
        gsmall_ref[2:3, :] += grad_read

        def spill(turn, carry):
            for inner in range(UNROLL):
                row = turn * UNROLL + inner
                at = pl.multiple_of(idx_ref[base + row], 4)
                rows[pl.ds(at, 4), :] = stage[pl.ds(pl.multiple_of(row * 4, 4), 4), :]
            return carry

        lax.fori_loop(0, total // UNROLL, spill, 0)

    @pl.when(step >= ins + blocks)
    def _():
        base = pl.multiple_of((step - ins - blocks) * (CHUNK * 4), CHUNK * 4)
        d_edges = jnp.concatenate(
            [rows[pl.ds(base + part, CHUNK, stride=4), :].astype(BF16) for part in range(4)], axis=1
        )
        gwide_ref[...] += dot_tn(d_edges, kept_ref[...])
        drows_ref[...] = dot_nn(d_edges, wide_ref[:, :H]).astype(BF16)

    @pl.when(step == ins + blocks + outs - 1)
    def _():
        shares = gwide_ref[:, :H] * wide_ref[:, :H].astype(F32)
        gsmall_ref[0:1, :] += jnp.sum(shares, axis=0, keepdims=True) / small_ref[0:1, :]
        size = mine_ref.shape[0]
        height = size // owners
        for owner in range(owners):
            for half in (0, 1):
                at = half * size + owner * height
                for ref, first, count, columns in packed_pieces(
                    owner, owners, gquery_ref, gwide_ref, ggateup_ref, gdown_ref, goutput_ref
                ):
                    for low in range(columns.start + half * LANES, columns.stop, H):
                        if low < ref.shape[1]:
                            rows[at : at + count, :] = ref[
                                first : first + count, low : low + LANES
                            ]
                        at += count
                rows[at : at + 8, :] = gsmall_ref[:, half * LANES : (half + 1) * LANES]
        core = core_ref[0]
        for ref, half in ((mine_ref, core), (theirs_ref, 1 - core)):
            ref[...] = rows[pl.ds(pl.multiple_of(half * size, 8), size), :].astype(BF16)


def packed_pieces(owner, owners, query, wide, gateup, down, output):
    count = 3 * H // owners
    first, last = owner * count, (owner + 1) * count
    if first < H:
        yield query, first, min(last, H) - first, range(H)
    if last > H:
        yield wide, max(first, H) - H, last - max(first, H), range(H)
    share = 2 * H // owners
    yield wide, owner * share, share, range(H, H + NB_ROWS)
    for ref in (gateup, down, output):
        share = ref.shape[0] // owners
        yield ref, owner * share, share, range(ref.shape[1])


def edges_backward(order_ref, rows_ref, src_ref, *rest):
    mine_ref, other_ref = rest[-2:]
    d_rows = rows_ref[...]
    source = src_ref[0]
    step = 256

    def sums(ref):
        for start in range(0, ref.shape[0], step):
            atom = lax.broadcasted_iota(jnp.int32, (step, 1), 0).astype(F32) + float(start)
            pick = jnp.where(atom == source, 1.0, 0.0).astype(BF16)
            ref[start : start + step, :] = dot_nn(pick, d_rows).astype(ref.dtype)

    pl.when(pl.program_id(0) == 0)(lambda: sums(mine_ref))
    pl.when(pl.program_id(0) == 1)(lambda: sums(other_ref))


def adamw_step(weight, first_mom, second, gradient, step_rate):
    first_new = BETA_ONE * first_mom + (1.0 - BETA_ONE) * gradient
    second_new = BETA_TWO * second + (1.0 - BETA_TWO) * gradient * gradient
    fix_one = 1.0 - BETA_ONE**STEP
    fix_two = 1.0 - BETA_TWO**STEP
    direction = first_new / fix_one / (jnp.sqrt(second_new / fix_two) + ADAM_EPS) + DECAY * weight
    return (first_new, second_new, weight - step_rate * direction)


def adamw_kernel(where_ref, held_ref, fetched_ref, *refs):
    ins, outs, lows = refs[:21], refs[21:42], refs[42:47]
    left, right = refs[47:]
    core = where_ref[0]
    for here in (0, 1):

        @pl.when(core == here)
        def _():
            for ref, half in ((held_ref, here), (fetched_ref, 1 - here)):
                (left, right)[half][...] = ref[...]

    def packed(at, rows, pieces=1):
        halves = [
            half[at + part * rows : at + (part + 1) * rows, :]
            for part in range(pieces)
            for half in (left, right)
        ]
        return jnp.concatenate(halves, axis=1)

    wa, wo, wd, wb = (ins[3 * number].shape[0] for number in (0, 1, 3, 4))
    wg = ins[6].shape[1]
    at = 0
    attention = packed(at, wa)
    at += wa
    basis = packed(at, wb, NB_ROWS // H)[:, :NB]
    at += wb * (NB_ROWS // H)
    gateup = packed(at, wg)
    if wg < LANES:
        gateup = jnp.concatenate([gateup, jnp.zeros((LANES - wg, H), F32)], axis=0)
    gateup = gateup.T[:, :wg]
    at += wg
    down = packed(at, wd, FF // H)
    at += wd * (FF // H)
    output = packed(at, wo)
    at += wo
    thin = packed(at, 8)
    width = ins[15].shape[1]
    column = lax.broadcasted_iota(jnp.int32, (H, width), 0)
    mine = lax.broadcasted_iota(jnp.int32, (H, width), 1) + where_ref[1] * width
    thin = jnp.dot(
        thin,
        jnp.where(column == mine, 1.0, 0.0),
        precision=lax.Precision.HIGHEST,
        preferred_element_type=F32,
    )
    gradients = (attention, output, gateup, down, basis, thin[2:3], thin[:2])
    rates = (H ** (-0.5), (H // 16) ** (-0.5), H ** (-0.5), FF ** (-0.5), 0.5, H ** (-0.5), 0.2)
    for number, (gradient, rate) in enumerate(zip(gradients, rates, strict=True)):
        weight, first, second = (ref[...] for ref in ins[3 * number : 3 * number + 3])
        results = adamw_step(weight, first, second, gradient, rate)
        for ref, value in zip(outs[3 * number : 3 * number + 3], results, strict=True):
            ref[...] = value
        if number < 5:
            lows[number][...] = results[2].astype(BF16)


def run_adamw(where, held, fetched, states):
    arrays = [array for triple in states for array in triple]
    spec = pl.BlockSpec(memory_space=pltpu.VMEM)
    shapes = [
        jax.ShapeDtypeStruct(array.shape, F32) for triple in states for array in (*triple[1:], triple[0])
    ]
    shapes += [jax.ShapeDtypeStruct(triple[0].shape, BF16) for triple in states[:5]]
    return list(
        pl.pallas_call(
            adamw_kernel,
            in_specs=[pl.BlockSpec(memory_space=pltpu.SMEM)] + [spec] * (2 + len(arrays)),
            out_specs=[spec] * len(shapes),
            out_shape=shapes,
            scratch_shapes=[pltpu.VMEM(held.shape, F32)] * 2,
            compiler_params=pltpu.CompilerParams(vmem_limit_bytes=VMEM_BYTES),
        )(where, held, fetched, *arrays)
    )


def whole_spec(shape):
    return pl.BlockSpec(shape, lambda *_: (0,) * len(shape), pipeline_mode=pl.Buffered(1))


def run_edges_forward(place, order, sources, small, dist_cols, src_cols, before):
    atoms = sources[0].shape[0]
    count = len(sources)
    owners, groups, _, columns = dist_cols.shape
    size = columns * LANES

    def picked(i, g, order_ref):
        return (order_ref[place + i], g, 0, 0)

    return pl.pallas_call(
        functools.partial(edges_forward, count),
        grid_spec=pltpu.PrefetchScalarGridSpec(
            num_scalar_prefetch=1,
            grid=(count, groups),
            in_specs=[
                whole_spec(small.shape),
                pl.BlockSpec((1, 1, LANES, columns), picked),
                pl.BlockSpec((1, 1, LANES, columns), picked),
            ]
            + [whole_spec(source.shape) for source in sources]
            + [pl.BlockSpec(memory_space=pl.ANY)] * len(before),
            out_specs=pl.BlockSpec(
                (size, WIDE), lambda i, g, order_ref: ((place + i) * groups + g, 0)
            ),
            scratch_shapes=[pltpu.VMEM((atoms, H), BF16)],
        ),
        out_shape=jax.ShapeDtypeStruct((owners * groups * size, WIDE), BF16),
        input_output_aliases={4 + count: 0} if before else {},
        compiler_params=pltpu.CompilerParams(vmem_limit_bytes=VMEM_BYTES),
        cost_estimate=pl.CostEstimate(
            flops=2 * count * groups * size * atoms * H,
            bytes_accessed=count * (groups * size * 2 * WIDE + atoms * H * 2),
            transcendentals=count * groups * size * NB_PAD,
        ),
    )(order, small, dist_cols, src_cols, *sources, *before)


def run_atoms(
    owners, idx, core, kept, features, cot, ecot, count, small, wide, query, output, gateup, down
):
    edges, atoms = kept.shape[0], features.shape[0]
    ins, blocks = edges // CHUNK, atoms // BLOCK
    outs = ins
    slots = edges // atoms
    ff = down.shape[1]
    height = (3 * H + 3 * 2 * H + gateup.shape[0] + ff // H * H + H) // owners + 8

    def atom_block(i):
        return (jnp.clip(i - ins, 0, blocks - 1), 0)

    def edge_block(i):
        return (jnp.where(i < ins, i, jnp.maximum(i - ins - blocks, 0)), 0)

    return pl.pallas_call(
        functools.partial(atoms_kernel, ins, blocks, outs, owners),
        grid=(ins + blocks + outs,),
        in_specs=[
            pl.BlockSpec(memory_space=pltpu.SMEM),
            pl.BlockSpec(memory_space=pltpu.SMEM),
            pl.BlockSpec((CHUNK, WIDE), edge_block),
            pl.BlockSpec((BLOCK, H), atom_block),
            pl.BlockSpec((BLOCK, H), atom_block),
            pl.BlockSpec((BLOCK, 1), atom_block),
            pl.BlockSpec((BLOCK, 1), atom_block),
            whole_spec(small.shape),
            whole_spec(wide.shape),
            whole_spec(query.shape),
            whole_spec(output.shape),
            whole_spec(gateup.shape),
            whole_spec(down.shape),
        ],
        out_specs=[
            pl.BlockSpec((BLOCK, H), atom_block),
            pl.BlockSpec((BLOCK, LANES), atom_block),
            pl.BlockSpec((BLOCK, H), atom_block),
            pl.BlockSpec((BLOCK, H), atom_block),
            pl.BlockSpec((CHUNK, H), lambda i: (jnp.maximum(i - ins - blocks, 0), 0)),
            whole_spec((owners * height, LANES)),
            whole_spec((owners * height, LANES)),
        ],
        out_shape=[
            jax.ShapeDtypeStruct((atoms, H), BF16),
            jax.ShapeDtypeStruct((atoms, LANES), F32),
            jax.ShapeDtypeStruct((atoms, H), F32),
            jax.ShapeDtypeStruct((atoms, H), F32),
            jax.ShapeDtypeStruct((edges, H), BF16),
            jax.ShapeDtypeStruct((owners * height, LANES), BF16),
            jax.ShapeDtypeStruct((owners * height, LANES), BF16),
        ],
        scratch_shapes=[
            pltpu.VMEM((edges * 4 + 8, LANES), F32),
            pltpu.VMEM((slots * BLOCK * 4 + 8, LANES), F32),
            pltpu.VMEM((BLOCK, slots * H), BF16),
            pltpu.VMEM((slots * HEADS, slots * H), BF16),
            pltpu.VMEM((slots * H, slots * HEADS), BF16),
            pltpu.VMEM(wide.shape, F32),
            pltpu.VMEM(gateup.shape, F32),
            pltpu.VMEM(down.shape, F32),
            pltpu.VMEM(output.shape, F32),
            pltpu.VMEM(query.shape, F32),
            pltpu.VMEM((8, H), F32),
        ],
        compiler_params=pltpu.CompilerParams(vmem_limit_bytes=VMEM_BYTES),
        cost_estimate=pl.CostEstimate(
            flops=2 * edges * H * (WIDE * 4 + H * 8) + 2 * atoms * H * ff * 9,
            bytes_accessed=edges * WIDE * 4 + edges * H * 2 + ff * H * 3 * 6,
            transcendentals=edges * HEADS,
        ),
    )(idx, core, kept, features, cot, ecot, count, small, wide, query, output, gateup, down)


def run_edges_backward(turn, order, d_rows, src_rows, atoms, after):
    owners, sent = src_rows.shape[0], src_rows.shape[2]
    return pl.pallas_call(
        edges_backward,
        grid_spec=pltpu.PrefetchScalarGridSpec(
            num_scalar_prefetch=1,
            grid=(2,),
            in_specs=[
                pl.BlockSpec((sent, H), lambda i, order_ref: (2 * turn + i, 0)),
                pl.BlockSpec((1, 1, sent), lambda i, order_ref: (order_ref[2 * turn + i], 0, 0)),
            ]
            + [pl.BlockSpec(memory_space=pl.ANY)] * len(after),
            out_specs=[whole_spec((atoms, H)), whole_spec((atoms, H))],
        ),
        out_shape=[jax.ShapeDtypeStruct((atoms, H), BF16)] * 2,
        compiler_params=pltpu.CompilerParams(vmem_limit_bytes=VMEM_BYTES),
        cost_estimate=pl.CostEstimate(
            flops=4 * sent * atoms * H,
            bytes_accessed=2 * sent * 2 * H + 4 * atoms * H,
            transcendentals=0,
        ),
    )(order, d_rows, src_rows, *after)


def halves(axis_size):
    return range((axis_size - 1).bit_length())


def across(array, bit):
    size = lax.axis_size("rep")
    return lax.ppermute(array, "rep", [(r, r ^ (1 << bit)) for r in range(size)])


def behind(array, other):
    return lax.optimization_barrier((array, other))[0]


def halve(totals, bit):
    half = totals.shape[1] // 2
    upper = (lax.axis_index("rep") >> bit) & 1
    sent = lax.dynamic_slice_in_dim(totals, (1 - upper) * half, half, 1)
    return lax.dynamic_slice_in_dim(totals, upper * half, half, 1), sent.astype(BF16)


def gather_back(held):
    reps = lax.axis_size("rep")
    me = lax.axis_index("rep")
    for bit in reversed(halves(reps)[1:]):
        fetched = across(held, bit)
        upper = (me >> bit) & 1 == 1
        held = jnp.concatenate(
            [jnp.where(upper, fetched, held), jnp.where(upper, held, fetched)], axis=0
        )
    return held, across(held, 0)


def ring_of(owners):
    pairs = owners // 2
    return [*range(0, pairs, 2), *reversed(range(1, pairs, 2))]


def ring_step(array):
    owners = lax.axis_size("edge")
    ring = ring_of(owners)
    moves = [
        (2 * here + side, 2 * ring[(at + 1) % len(ring)] + side)
        for at, here in enumerate(ring)
        for side in (0, 1)
    ]
    return lax.ppermute(array, "edge", moves)


def pair_swap(array):
    owners = lax.axis_size("edge")
    return lax.ppermute(array, "edge", [(e, e ^ 1) for e in range(owners)])


def arrival_order(owners):
    ring = ring_of(owners)
    table = np.zeros((owners, owners), np.int32)
    for at, here in enumerate(ring):
        for side in (0, 1):
            for turn in range(len(ring)):
                source = 2 * ring[at - turn]
                table[2 * here + side, 2 * turn : 2 * turn + 2] = (source + side, source + 1 - side)
    return table


def local(
    atom_features,
    distances,
    source_index,
    slot_index,
    live_mask,
    output_cot,
    energy_cot,
    attention_weight,
    attention_first,
    attention_second,
    output_weight,
    output_first,
    output_second,
    gateup_weight,
    gateup_first,
    gateup_second,
    down_weight,
    down_first,
    down_second,
    basis_weight,
    basis_first,
    basis_second,
    readout_weight,
    readout_first,
    readout_second,
    norm_gains,
    gains_first,
    gains_second,
):
    features = atom_features[0]
    atoms = features.shape[0]
    slots = slot_index.shape[2]
    edges = atoms * slots
    owners = H // output_weight.shape[1]
    sent = edges // owners
    wa, wo, wg, wd, wb, wr = (
        attention_weight.shape[1],
        output_weight.shape[1],
        gateup_weight.shape[1],
        down_weight.shape[1],
        basis_weight.shape[1],
        readout_weight.shape[0],
    )

    dist = distances[0]
    high = lax.reduce_precision(dist, 8, 7)
    middle = lax.reduce_precision(dist - high, 8, 7)
    lower = dist - high - middle
    source = source_index[0]
    pieces = (high, middle, lower, source >> 5, source & 31)
    meta = jnp.stack([piece.astype(BF16) for piece in pieces])
    meta = meta.reshape(5, owners, sent // H, H).transpose(1, 0, 2, 3)
    meta_rows = 5 * sent // H
    thin = jnp.concatenate([norm_gains, readout_weight[None]], axis=0).astype(BF16).reshape(1, 1, -1)
    thin = jnp.broadcast_to(
        jnp.pad(thin, ((0, 0), (0, 7), (0, H - thin.shape[2]))), (owners, 8, H)
    )
    meta = jnp.concatenate([meta.reshape(owners, meta_rows, H), thin], axis=1)
    meta = lax.all_to_all(meta, "edge", 0, 0, tiled=True)
    small = meta[:, meta_rows, : 3 * wr].reshape(owners, 3, wr)
    small = small.transpose(1, 0, 2).reshape(3, H)
    small = jnp.pad(small.astype(F32), ((0, 5), (0, 0)))
    pieces = meta[:, :meta_rows].reshape(owners, 5, sent).astype(F32)
    dist = pieces[:, 0] + pieces[:, 1] + pieces[:, 2]
    source = pieces[:, 3] * 32.0 + pieces[:, 4]

    basis_rows = jnp.pad(basis_weight.T.astype(BF16), ((0, 0), (0, NB_ROWS - NB)))
    weight_rows = jnp.concatenate(
        [
            attention_weight.T.astype(BF16),
            basis_rows.reshape(3 * wb, H),
            gateup_weight.T.astype(BF16),
            down_weight.T.astype(BF16).reshape(wd * (FF // H), H),
            output_weight.T.astype(BF16),
        ],
        axis=0,
    )
    weight_rows = lax.all_gather(weight_rows, "edge", axis=0)
    at = 0
    fulls = []
    for width, rows in ((H, wa), (NB_ROWS, wb), (H, wg), (FF, wd), (H, wo)):
        count = rows * width // H
        fulls.append(weight_rows[:, at : at + count].reshape(owners * rows, width))
        at += count
    attention_rows, basis_rows, gateup_rows, down_rows, output_rows = fulls
    query_rows, kv_rows = attention_rows[:H], attention_rows[H:]
    wide = jnp.concatenate([kv_rows, basis_rows[:, :NB_PAD]], axis=1)

    size = min(GROUP, sent)
    dist_cols, src_cols = (
        values.reshape(owners, sent // size, size // LANES, LANES).transpose(0, 1, 3, 2)
        for values in (dist, source)
    )
    src_rows = source[:, None]

    table = arrival_order(owners)
    me = lax.axis_index("edge")
    order = jnp.asarray(table)[me]
    place = jnp.asarray(np.argsort(table, axis=1).astype(np.int32))[me]
    turns = owners // 2
    arrivals = [features]
    if turns > 1:
        arrivals.append(ring_step(features))
    swapped = [pair_swap(array) for array in arrivals]
    ahead = ring_step(arrivals[1]) if turns > 2 else None
    kept = run_edges_forward(0, order, [features], small, dist_cols, src_cols, ())
    kept = run_edges_forward(1, order, [swapped[0]], small, dist_cols, src_cols, (kept,))
    if turns > 1:
        sources = [arrivals[1], swapped[1]]
        if turns > 2:
            ahead, kept = lax.optimization_barrier((ahead, kept))
        kept = run_edges_forward(2, order, sources, small, dist_cols, src_cols, (kept,))
    for turn in range(2, turns):
        sources = [ahead, pair_swap(ahead)]
        if turn < turns - 1:
            ahead, kept = lax.optimization_barrier((ring_step(ahead), kept))
        kept = run_edges_forward(2 * turn, order, sources, small, dist_cols, src_cols, (kept,))

    slot_ids = slot_index[0]
    slot_owner = slot_ids // sent
    arrived = sum(jnp.where(slot_owner == s, place[s], 0) for s in range(owners))
    arrived = arrived * sent + slot_ids % sent
    idx = arrived.reshape(atoms // BLOCK, BLOCK, slots).transpose(0, 2, 1).reshape(-1) * 4
    count = jnp.sum(live_mask[0], axis=1, keepdims=True).astype(F32)
    core = (lax.axis_index("rep") & 1).astype(jnp.int32)[None]
    block_out, energy, d_after, d_normed_own, d_rows, grads_mine, grads_theirs = run_atoms(
        owners,
        idx,
        core,
        kept,
        features,
        output_cot[0],
        energy_cot[0][:, None],
        count,
        small,
        wide,
        query_rows,
        output_rows,
        gateup_rows,
        down_rows,
    )
    turns_back = [*range(1, turns), 0]
    bits = halves(lax.axis_size("rep"))[1:]
    fetched = across(grads_theirs, 0)
    parts, after, running = [], (), None

    def add_pair(number, latest):
        part, other = parts[number]
        if running is None:
            return part.astype(F32) + behind(other, latest).astype(F32)
        moved = behind(ring_step(running), latest)
        return part.astype(F32) + other.astype(F32) + moved.astype(F32)

    for number, turn in enumerate(turns_back):
        part, part_other = run_edges_backward(turn, order, d_rows, src_rows, atoms, after)
        parts.append((part, pair_swap(part_other)))
        after = ()
        if number == 1:
            totals = grads_mine.astype(F32) + behind(fetched, part).astype(F32)
            totals, sent_rows = halve(totals.reshape(owners, -1, LANES), bits[0])
            fetched = across(sent_rows, bits[0])
            after = (sent_rows,)
        elif 1 < number < turns - 1:
            running = add_pair(number - 2, part).astype(BF16)
            after = (running,)
    totals = totals + behind(fetched, part).astype(F32)
    for bit in bits[1:]:
        totals, sent_rows = halve(totals, bit)
        totals = totals + across(sent_rows, bit).astype(F32)
    totals = totals.astype(BF16)
    pieces = lax.all_to_all(totals, "edge", 0, 0, tiled=True)
    latest = totals
    for number in range(turns - 3, turns):
        if number == turns - 1:
            latest = held = jnp.sum(pieces.astype(F32), axis=0)
        total = add_pair(number, latest)
        running = total.astype(BF16)
    d_from_edges = total
    held, fetched = gather_back(held)

    features = features.astype(F32)
    inv_one = inverse_rms(features)
    d_normed_one = d_normed_own + d_from_edges
    scaled = d_normed_one * small[0:1]
    input_grad = (
        d_after
        + inv_one * scaled
        - features * inv_one**3 * jnp.mean(scaled * features, axis=-1, keepdims=True)
    )

    where = jnp.stack([core[0], me.astype(jnp.int32)])
    states = (
        (attention_weight, attention_first, attention_second),
        (output_weight, output_first, output_second),
        (gateup_weight, gateup_first, gateup_second),
        (down_weight, down_first, down_second),
        (basis_weight, basis_first, basis_second),
        (readout_weight, readout_first, readout_second),
        (norm_gains, gains_first, gains_second),
    )

    def turn_over(number, array):
        return array.T if number in (0, 1, 3, 4) else array[None] if number == 5 else array

    updated = run_adamw(
        where,
        held,
        fetched,
        [[turn_over(number, array) for array in triple] for number, triple in enumerate(states)],
    )
    flat = [
        array[0] if at // 3 == 5 else turn_over(at // 3, array)
        for at, array in enumerate(updated[:21])
    ]
    lows = [turn_over(number, array) for number, array in enumerate(updated[21:])]
    return (block_out[None], energy[:, 0][None], input_grad[None], *flat, *lows)


def solution(mesh):
    matrix = P(None, "edge")
    rows = P("rep", "edge", None)
    pairs = P("rep", "edge")
    weights = (matrix,) * 15 + (P("edge"),) * 3 + (matrix,) * 3
    return jax.shard_map(
        local,
        mesh=mesh,
        in_specs=(rows, pairs, pairs, rows, rows, rows, pairs) + weights,
        out_specs=(rows, pairs, rows) + weights + (matrix,) * 5,
        check_vma=False,
    )
```

```python
import functools
import math

import jax
import jax.numpy as jnp
import numpy as np
from jax import lax
from jax.experimental import pallas as pl
from jax.experimental.pallas import tpu as pltpu
from jax.sharding import PartitionSpec as P

H = 256
HEADS = 8
FF = 1024
NB = 600
STEP = 5
HEAD_DIM = 32

EPS = 1e-06
CUTOFF = 6.0
BETA_ONE = 0.5
BETA_TWO = 0.5
ADAM_EPS = 1e-08
DECAY = 0.01

LANES = 128
NB_PAD = 640
NB_ROWS = 768
WIDE = H + NB_PAD
CHUNK = 1024
BLOCK = 128
GROUP = 1024
UNROLL = 16
STRIDE = 5
VMEM_BYTES = 60 * 1024 * 1024

F32 = jnp.float32
BF16 = jnp.bfloat16


def dot_nn(left, right):
    return jnp.dot(left, right, preferred_element_type=F32)


def dot_nt(left, right):
    return lax.dot_general(left, right, (((1,), (1,)), ((), ())), preferred_element_type=F32)


def dot_tn(left, right):
    return lax.dot_general(left, right, (((0,), (0,)), ((), ())), preferred_element_type=F32)


def inverse_rms(rows):
    return lax.rsqrt(jnp.mean(rows * rows, axis=-1, keepdims=True) + EPS)


def edges_forward(count, order_ref, small_ref, dist_ref, src_ref, *rest):
    feature_refs, (kept_ref, normed_ref) = rest[:count], rest[-2:]
    atoms = normed_ref.shape[0]

    def norm(ref):
        features = ref[...].astype(F32)
        normed_ref[...] = (features * inverse_rms(features) * small_ref[0:1, :]).astype(BF16)

    first = pl.program_id(1) == 0
    for number, ref in enumerate(feature_refs):
        pl.when(jnp.logical_and(first, pl.program_id(0) == number))(functools.partial(norm, ref))
    atom_lane = lax.broadcasted_iota(jnp.int32, (1, atoms), 1).astype(F32)
    centres = lax.broadcasted_iota(jnp.int32, (1, NB_PAD), 1).astype(F32) * (CUTOFF / (NB - 1))
    per_spread = math.sqrt(math.log2(math.e)) / (2.0 * CUTOFF / (NB - 1))
    picks, bases = [], []
    for column in range(dist_ref.shape[3]):
        source = src_ref[0, 0, :, column : column + 1]
        picks.append(jnp.where(source == atom_lane, 1.0, 0.0).astype(BF16))
        offset = (dist_ref[0, 0, :, column : column + 1] - centres) * per_spread
        bases.append(jnp.exp2(-(offset * offset)).astype(BF16))
    kept_ref[:, :H] = dot_nn(jnp.concatenate(picks, axis=0), normed_ref[...]).astype(BF16)
    kept_ref[:, H:] = jnp.concatenate(bases, axis=0)


def atoms_kernel(
    ins, blocks, outs, owners,
    idx_ref, core_ref, kept_ref, x_ref, cot_ref, ecot_ref, count_ref, small_ref,
    wide_ref, query_ref, output_ref, gateup_ref, down_ref,
    block_ref, energy_ref, after_ref, dnorm_ref, drows_ref, mine_ref, theirs_ref,
    rows, stage, products, spread_out, sum_up,
    gwide_ref, ggateup_ref, gdown_ref, goutput_ref, gquery_ref, gsmall_ref,
):
    step = pl.program_id(0)
    scaling = HEAD_DIM ** (-0.5)
    slots = stage.shape[0] // (STRIDE * BLOCK)
    pairs = slots * HEADS

    @pl.when(step == 0)
    def _():
        for ref in (gwide_ref, ggateup_ref, gdown_ref, goutput_ref, gquery_ref, gsmall_ref):
            ref[...] = jnp.zeros_like(ref)
        lane = lax.broadcasted_iota(jnp.int32, (pairs, slots * H), 1) // HEAD_DIM
        pair = lax.broadcasted_iota(jnp.int32, (pairs, slots * H), 0)
        spread_out[...] = jnp.where(lane == pair, 1.0, 0.0).astype(BF16)
        lane = lax.broadcasted_iota(jnp.int32, (slots * H, pairs), 0) // HEAD_DIM
        pair = lax.broadcasted_iota(jnp.int32, (slots * H, pairs), 1)
        sum_up[...] = jnp.where(lane == pair, 1.0, 0.0).astype(BF16)

    @pl.when(step < ins)
    def _():
        base = pl.multiple_of(step * (CHUNK * 4), CHUNK * 4)
        edge_kv = dot_nt(kept_ref[...], wide_ref[...]).astype(BF16).astype(F32)
        for part in range(4):
            rows[pl.ds(base + part, CHUNK, stride=4), :] = edge_kv[
                :, part * LANES : (part + 1) * LANES
            ]

    @pl.when(jnp.logical_and(step >= ins, step < ins + blocks))
    def _():
        block = step - ins
        total = slots * BLOCK
        base = block * total

        def fetch(turn, carry):
            for inner in range(UNROLL):
                row = turn * UNROLL + inner
                at = pl.multiple_of(idx_ref[base + row], 4)
                stage[pl.ds(row * STRIDE, 4), :] = rows[pl.ds(at, 4), :]
            return carry

        lax.fori_loop(0, total // UNROLL, fetch, 0)

        def staged(slot, part):
            first = slot * (STRIDE * BLOCK) + 2 * part
            return jnp.concatenate(
                [stage[pl.ds(first + half, BLOCK, stride=STRIDE), :] for half in (0, 1)], axis=1
            )

        def put(slot, part, value):
            first = slot * (STRIDE * BLOCK) + 2 * part
            for half in (0, 1):
                stage[pl.ds(first + half, BLOCK, stride=STRIDE), :] = value[
                    :, half * LANES : (half + 1) * LANES
                ]

        def over_slots(values, combine):
            shift = HEADS
            while shift < pairs:
                values = combine(values, pltpu.roll(values, shift, 1))
                shift *= 2
            return values

        def over_features(left, part):
            for slot in range(slots):
                products[:, slot * H : (slot + 1) * H] = (left * staged(slot, part)).astype(BF16)
            return dot_nn(products[...], sum_up[...])

        gain_one = small_ref[0:1, :]
        gain_two = small_ref[1:2, :]
        reader = small_ref[2:3, :]
        features = x_ref[...].astype(F32)
        inv_one = inverse_rms(features)
        normed_one = (features * inv_one * gain_one).astype(BF16)
        queries = dot_nt(normed_one, query_ref[...]).astype(BF16).astype(F32)

        scores = over_features(queries, 0) * scaling
        slot_of = lax.broadcasted_iota(jnp.int32, (1, pairs), 1) // HEADS
        scores = jnp.where(slot_of.astype(F32) < count_ref[...], scores, -1e30)
        terms = jnp.exp(scores - over_slots(scores, jnp.maximum))
        soft = terms / over_slots(terms, jnp.add)
        soft_low = soft.astype(BF16)

        def spread(values, slot):
            return dot_nn(values, spread_out[:, slot * H : (slot + 1) * H])

        mixture = jnp.zeros((BLOCK, H), F32)
        for slot in range(slots):
            mixture += spread(soft_low, slot) * staged(slot, 1)
        mixture = mixture.astype(BF16)

        after = features + dot_nt(mixture, output_ref[...])
        inv_two = inverse_rms(after)
        normed_two = (after * inv_two * gain_two).astype(BF16)
        gate_up = dot_nt(normed_two, gateup_ref[...])
        ff = gate_up.shape[1] // 2
        gate, up_part = gate_up[:, :ff], gate_up[:, ff:]
        gate_sig = 1.0 / (1.0 + jnp.exp(-gate))
        swished = gate * gate_sig
        hidden = (swished * up_part).astype(BF16)
        result = after + dot_nt(hidden, down_ref[...])
        block_ref[...] = result.astype(BF16)
        energy_ref[...] = jnp.broadcast_to(
            jnp.sum(result * reader, axis=-1, keepdims=True), energy_ref.shape
        )
        energy_row = ecot_ref[...]
        d_result = cot_ref[...].astype(F32) + energy_row * reader
        grad_read = jnp.sum(energy_row * result, axis=0, keepdims=True)
        d_ffn = d_result.astype(BF16)
        gdown_ref[...] += dot_tn(d_ffn, hidden)
        d_hidden = dot_nn(d_ffn, down_ref[...])
        d_gate = d_hidden * up_part * gate_sig * (1.0 + gate * (1.0 - gate_sig))
        d_gate_up = jnp.concatenate(
            [d_gate.astype(BF16), (d_hidden * swished).astype(BF16)], axis=1
        )
        ggateup_ref[...] += dot_tn(d_gate_up, normed_two)
        d_normed_two = dot_nn(d_gate_up, gateup_ref[...])
        scaled = d_normed_two * gain_two
        grad_gain_two = jnp.sum(d_normed_two * after * inv_two, axis=0, keepdims=True)
        d_after = (
            d_result
            + inv_two * scaled
            - after * (inv_two * inv_two * inv_two)
            * jnp.mean(scaled * after, axis=-1, keepdims=True)
        )
        after_ref[...] = d_after
        d_attn = d_after.astype(BF16)
        goutput_ref[...] += dot_tn(d_attn, mixture)
        d_mixture = dot_nn(d_attn, output_ref[...]).astype(BF16).astype(F32)

        d_soft = over_features(d_mixture, 1)
        d_scores = soft * (d_soft - over_slots(soft * d_soft, jnp.add))
        d_scores = d_scores.astype(BF16)
        scaled_queries = queries * scaling
        d_queries = jnp.zeros((BLOCK, H), F32)
        for slot in range(slots):
            wide_scores = spread(d_scores, slot)
            d_queries += wide_scores * staged(slot, 0)
            put(slot, 0, wide_scores * scaled_queries)
            put(slot, 1, spread(soft_low, slot) * d_mixture)
        d_queries = (d_queries * scaling).astype(BF16)
        gquery_ref[...] += dot_tn(d_queries, normed_one)
        d_normed = dot_nn(d_queries, query_ref[...])
        dnorm_ref[...] = d_normed
        grad_gain_one = jnp.sum(d_normed * features * inv_one, axis=0, keepdims=True)
        gsmall_ref[0:1, :] += grad_gain_one
        gsmall_ref[1:2, :] += grad_gain_two
        gsmall_ref[2:3, :] += grad_read

        def spill(turn, carry):
            for inner in range(UNROLL):
                row = turn * UNROLL + inner
                at = pl.multiple_of(idx_ref[base + row], 4)
                rows[pl.ds(at, 4), :] = stage[pl.ds(row * STRIDE, 4), :]
            return carry

        lax.fori_loop(0, total // UNROLL, spill, 0)

    @pl.when(step >= ins + blocks)
    def _():
        base = pl.multiple_of((step - ins - blocks) * (CHUNK * 4), CHUNK * 4)
        d_edges = jnp.concatenate(
            [rows[pl.ds(base + part, CHUNK, stride=4), :].astype(BF16) for part in range(4)], axis=1
        )
        gwide_ref[...] += dot_tn(d_edges, kept_ref[...])
        drows_ref[...] = dot_nn(d_edges, wide_ref[:, :H]).astype(BF16)

    @pl.when(step == ins + blocks + outs - 1)
    def _():
        shares = gwide_ref[:, :H] * wide_ref[:, :H].astype(F32)
        gsmall_ref[0:1, :] += jnp.sum(shares, axis=0, keepdims=True) / small_ref[0:1, :]
        size = mine_ref.shape[0]
        height = size // owners
        for owner in range(owners):
            for half in (0, 1):
                at = half * size + owner * height
                for ref, first, count, columns in packed_pieces(
                    owner, owners, gquery_ref, gwide_ref, ggateup_ref, gdown_ref, goutput_ref
                ):
                    for low in range(columns.start + half * LANES, columns.stop, H):
                        if low < ref.shape[1]:
                            rows[at : at + count, :] = ref[
                                first : first + count, low : low + LANES
                            ]
                        at += count
                rows[at : at + 8, :] = gsmall_ref[:, half * LANES : (half + 1) * LANES]
        core = core_ref[0]
        for ref, half in ((mine_ref, core), (theirs_ref, 1 - core)):
            ref[...] = rows[pl.ds(pl.multiple_of(half * size, 8), size), :].astype(BF16)


def packed_pieces(owner, owners, query, wide, gateup, down, output):
    count = 3 * H // owners
    first, last = owner * count, (owner + 1) * count
    if first < H:
        yield query, first, min(last, H) - first, range(H)
    if last > H:
        yield wide, max(first, H) - H, last - max(first, H), range(H)
    share = 2 * H // owners
    yield wide, owner * share, share, range(H, H + NB_ROWS)
    for ref in (gateup, down, output):
        share = ref.shape[0] // owners
        yield ref, owner * share, share, range(ref.shape[1])


def edges_backward(order_ref, rows_ref, src_ref, *rest):
    mine_ref, other_ref = rest[-2:]
    d_rows = rows_ref[...]
    source = src_ref[0]
    step = 256

    def sums(ref):
        for start in range(0, ref.shape[0], step):
            atom = lax.broadcasted_iota(jnp.int32, (step, 1), 0).astype(F32) + float(start)
            pick = jnp.where(atom == source, 1.0, 0.0).astype(BF16)
            ref[start : start + step, :] = dot_nn(pick, d_rows).astype(ref.dtype)

    pl.when(pl.program_id(0) == 0)(lambda: sums(mine_ref))
    pl.when(pl.program_id(0) == 1)(lambda: sums(other_ref))


def adamw_step(weight, first_mom, second, gradient, step_rate):
    first_new = BETA_ONE * first_mom + (1.0 - BETA_ONE) * gradient
    second_new = BETA_TWO * second + (1.0 - BETA_TWO) * gradient * gradient
    fix_one = 1.0 - BETA_ONE**STEP
    fix_two = 1.0 - BETA_TWO**STEP
    direction = first_new / fix_one / (jnp.sqrt(second_new / fix_two) + ADAM_EPS) + DECAY * weight
    return (first_new, second_new, weight - step_rate * direction)


def adamw_kernel(where_ref, held_ref, fetched_ref, *refs):
    ins, outs, lows = refs[:21], refs[21:42], refs[42:47]
    left, right = refs[47:]
    core = where_ref[0]
    for here in (0, 1):

        @pl.when(core == here)
        def _():
            for ref, half in ((held_ref, here), (fetched_ref, 1 - here)):
                (left, right)[half][...] = ref[...]

    def packed(at, rows, pieces=1):
        halves = [
            half[at + part * rows : at + (part + 1) * rows, :]
            for part in range(pieces)
            for half in (left, right)
        ]
        return jnp.concatenate(halves, axis=1)

    wa, wo, wd, wb = (ins[3 * number].shape[0] for number in (0, 1, 3, 4))
    wg = ins[6].shape[1]
    at = 0
    attention = packed(at, wa)
    at += wa
    basis = packed(at, wb, NB_ROWS // H)[:, :NB]
    at += wb * (NB_ROWS // H)
    gateup = packed(at, wg)
    if wg < LANES:
        gateup = jnp.concatenate([gateup, jnp.zeros((LANES - wg, H), F32)], axis=0)
    gateup = gateup.T[:, :wg]
    at += wg
    down = packed(at, wd, FF // H)
    at += wd * (FF // H)
    output = packed(at, wo)
    at += wo
    thin = packed(at, 8)
    width = ins[15].shape[1]
    column = lax.broadcasted_iota(jnp.int32, (H, width), 0)
    mine = lax.broadcasted_iota(jnp.int32, (H, width), 1) + where_ref[1] * width
    thin = jnp.dot(
        thin,
        jnp.where(column == mine, 1.0, 0.0),
        precision=lax.Precision.HIGHEST,
        preferred_element_type=F32,
    )
    gradients = (attention, output, gateup, down, basis, thin[2:3], thin[:2])
    rates = (H ** (-0.5), (H // 16) ** (-0.5), H ** (-0.5), FF ** (-0.5), 0.5, H ** (-0.5), 0.2)
    for number, (gradient, rate) in enumerate(zip(gradients, rates, strict=True)):
        weight, first, second = (ref[...] for ref in ins[3 * number : 3 * number + 3])
        results = adamw_step(weight, first, second, gradient, rate)
        for ref, value in zip(outs[3 * number : 3 * number + 3], results, strict=True):
            ref[...] = value
        if number < 5:
            lows[number][...] = results[2].astype(BF16)


def run_adamw(where, held, fetched, states):
    arrays = [array for triple in states for array in triple]
    spec = pl.BlockSpec(memory_space=pltpu.VMEM)
    shapes = [
        jax.ShapeDtypeStruct(array.shape, F32) for triple in states for array in (*triple[1:], triple[0])
    ]
    shapes += [jax.ShapeDtypeStruct(triple[0].shape, BF16) for triple in states[:5]]
    return list(
        pl.pallas_call(
            adamw_kernel,
            in_specs=[pl.BlockSpec(memory_space=pltpu.SMEM)] + [spec] * (2 + len(arrays)),
            out_specs=[spec] * len(shapes),
            out_shape=shapes,
            scratch_shapes=[pltpu.VMEM(held.shape, F32)] * 2,
            compiler_params=pltpu.CompilerParams(vmem_limit_bytes=VMEM_BYTES),
        )(where, held, fetched, *arrays)
    )


def whole_spec(shape):
    return pl.BlockSpec(shape, lambda *_: (0,) * len(shape), pipeline_mode=pl.Buffered(1))


def run_edges_forward(place, order, sources, small, dist_cols, src_cols, before):
    atoms = sources[0].shape[0]
    count = len(sources)
    owners, groups, _, columns = dist_cols.shape
    size = columns * LANES

    def picked(i, g, order_ref):
        return (order_ref[place + i], g, 0, 0)

    return pl.pallas_call(
        functools.partial(edges_forward, count),
        grid_spec=pltpu.PrefetchScalarGridSpec(
            num_scalar_prefetch=1,
            grid=(count, groups),
            in_specs=[
                whole_spec(small.shape),
                pl.BlockSpec((1, 1, LANES, columns), picked),
                pl.BlockSpec((1, 1, LANES, columns), picked),
            ]
            + [whole_spec(source.shape) for source in sources]
            + [pl.BlockSpec(memory_space=pl.ANY)] * len(before),
            out_specs=pl.BlockSpec(
                (size, WIDE), lambda i, g, order_ref: ((place + i) * groups + g, 0)
            ),
            scratch_shapes=[pltpu.VMEM((atoms, H), BF16)],
        ),
        out_shape=jax.ShapeDtypeStruct((owners * groups * size, WIDE), BF16),
        input_output_aliases={4 + count: 0} if before else {},
        compiler_params=pltpu.CompilerParams(vmem_limit_bytes=VMEM_BYTES),
        cost_estimate=pl.CostEstimate(
            flops=2 * count * groups * size * atoms * H,
            bytes_accessed=count * (groups * size * 2 * WIDE + atoms * H * 2),
            transcendentals=count * groups * size * NB_PAD,
        ),
    )(order, small, dist_cols, src_cols, *sources, *before)


def run_atoms(
    owners, idx, core, kept, features, cot, ecot, count, small, wide, query, output, gateup, down
):
    edges, atoms = kept.shape[0], features.shape[0]
    ins, blocks = edges // CHUNK, atoms // BLOCK
    outs = ins
    slots = edges // atoms
    ff = down.shape[1]
    height = (3 * H + 3 * 2 * H + gateup.shape[0] + ff // H * H + H) // owners + 8

    def atom_block(i):
        return (jnp.clip(i - ins, 0, blocks - 1), 0)

    def edge_block(i):
        return (jnp.where(i < ins, i, jnp.maximum(i - ins - blocks, 0)), 0)

    return pl.pallas_call(
        functools.partial(atoms_kernel, ins, blocks, outs, owners),
        grid=(ins + blocks + outs,),
        in_specs=[
            pl.BlockSpec(memory_space=pltpu.SMEM),
            pl.BlockSpec(memory_space=pltpu.SMEM),
            pl.BlockSpec((CHUNK, WIDE), edge_block),
            pl.BlockSpec((BLOCK, H), atom_block),
            pl.BlockSpec((BLOCK, H), atom_block),
            pl.BlockSpec((BLOCK, 1), atom_block),
            pl.BlockSpec((BLOCK, 1), atom_block),
            whole_spec(small.shape),
            whole_spec(wide.shape),
            whole_spec(query.shape),
            whole_spec(output.shape),
            whole_spec(gateup.shape),
            whole_spec(down.shape),
        ],
        out_specs=[
            pl.BlockSpec((BLOCK, H), atom_block),
            pl.BlockSpec((BLOCK, LANES), atom_block),
            pl.BlockSpec((BLOCK, H), atom_block),
            pl.BlockSpec((BLOCK, H), atom_block),
            pl.BlockSpec((CHUNK, H), lambda i: (jnp.maximum(i - ins - blocks, 0), 0)),
            whole_spec((owners * height, LANES)),
            whole_spec((owners * height, LANES)),
        ],
        out_shape=[
            jax.ShapeDtypeStruct((atoms, H), BF16),
            jax.ShapeDtypeStruct((atoms, LANES), F32),
            jax.ShapeDtypeStruct((atoms, H), F32),
            jax.ShapeDtypeStruct((atoms, H), F32),
            jax.ShapeDtypeStruct((edges, H), BF16),
            jax.ShapeDtypeStruct((owners * height, LANES), BF16),
            jax.ShapeDtypeStruct((owners * height, LANES), BF16),
        ],
        scratch_shapes=[
            pltpu.VMEM((edges * 4 + 8, LANES), F32),
            pltpu.VMEM((slots * BLOCK * STRIDE + 8, LANES), F32),
            pltpu.VMEM((BLOCK, slots * H), BF16),
            pltpu.VMEM((slots * HEADS, slots * H), BF16),
            pltpu.VMEM((slots * H, slots * HEADS), BF16),
            pltpu.VMEM(wide.shape, F32),
            pltpu.VMEM(gateup.shape, F32),
            pltpu.VMEM(down.shape, F32),
            pltpu.VMEM(output.shape, F32),
            pltpu.VMEM(query.shape, F32),
            pltpu.VMEM((8, H), F32),
        ],
        compiler_params=pltpu.CompilerParams(vmem_limit_bytes=VMEM_BYTES),
        cost_estimate=pl.CostEstimate(
            flops=2 * edges * H * (WIDE * 4 + H * 8) + 2 * atoms * H * ff * 9,
            bytes_accessed=edges * WIDE * 4 + edges * H * 2 + ff * H * 3 * 6,
            transcendentals=edges * HEADS,
        ),
    )(idx, core, kept, features, cot, ecot, count, small, wide, query, output, gateup, down)


def run_edges_backward(turn, order, d_rows, src_rows, atoms, after):
    owners, sent = src_rows.shape[0], src_rows.shape[2]
    return pl.pallas_call(
        edges_backward,
        grid_spec=pltpu.PrefetchScalarGridSpec(
            num_scalar_prefetch=1,
            grid=(2,),
            in_specs=[
                pl.BlockSpec((sent, H), lambda i, order_ref: (2 * turn + i, 0)),
                pl.BlockSpec((1, 1, sent), lambda i, order_ref: (order_ref[2 * turn + i], 0, 0)),
            ]
            + [pl.BlockSpec(memory_space=pl.ANY)] * len(after),
            out_specs=[whole_spec((atoms, H)), whole_spec((atoms, H))],
        ),
        out_shape=[jax.ShapeDtypeStruct((atoms, H), BF16)] * 2,
        compiler_params=pltpu.CompilerParams(vmem_limit_bytes=VMEM_BYTES),
        cost_estimate=pl.CostEstimate(
            flops=4 * sent * atoms * H,
            bytes_accessed=2 * sent * 2 * H + 4 * atoms * H,
            transcendentals=0,
        ),
    )(order, d_rows, src_rows, *after)


def halves(axis_size):
    return range((axis_size - 1).bit_length())


def across(array, bit):
    size = lax.axis_size("rep")
    return lax.ppermute(array, "rep", [(r, r ^ (1 << bit)) for r in range(size)])


def first_exchange(held):
    bit = halves(lax.axis_size("rep"))[-1]
    return {0: held, 1 << bit: across(held, bit)}


def share_rows(shares):
    reps = lax.axis_size("rep")
    me = lax.axis_index("rep")
    held = shares[0]
    for bit in reversed(halves(reps)[:-1]):
        shares = shares | {
            number | (1 << bit): across(array, bit) for number, array in shares.items()
        }
    ordered = []
    for batch in range(reps):
        share = held
        for number in range(1, reps):
            share = jnp.where(me ^ batch == number, shares[number], share)
        ordered.append(share)
    return jnp.concatenate(ordered, axis=1)


def behind(array, other):
    return lax.optimization_barrier((array, other))[0]


def halve(totals, bit):
    half = totals.shape[1] // 2
    upper = (lax.axis_index("rep") >> bit) & 1
    sent = lax.dynamic_slice_in_dim(totals, (1 - upper) * half, half, 1)
    return lax.dynamic_slice_in_dim(totals, upper * half, half, 1), sent.astype(BF16)


def ring_rows(totals, order, turns, running):
    for turn in turns:
        total = lax.dynamic_index_in_dim(totals, order[2 * turn] >> 1, 0, keepdims=False)
        if running is not None:
            total = total + ring_step(running.astype(BF16)).astype(F32)
        running = total
    return running


def gather_back(held):
    reps = lax.axis_size("rep")
    me = lax.axis_index("rep")
    for bit in reversed(halves(reps)[1:]):
        fetched = across(held, bit)
        upper = (me >> bit) & 1 == 1
        held = jnp.concatenate(
            [jnp.where(upper, fetched, held), jnp.where(upper, held, fetched)], axis=0
        )
    return held, across(held, 0)


def ring_of(owners):
    pairs = owners // 2
    return [*range(0, pairs, 2), *reversed(range(1, pairs, 2))]


def ring_step(array):
    owners = lax.axis_size("edge")
    ring = ring_of(owners)
    moves = [
        (2 * here + side, 2 * ring[(at + 1) % len(ring)] + side)
        for at, here in enumerate(ring)
        for side in (0, 1)
    ]
    return lax.ppermute(array, "edge", moves)


def pair_swap(array):
    owners = lax.axis_size("edge")
    return lax.ppermute(array, "edge", [(e, e ^ 1) for e in range(owners)])


def arrival_order(owners):
    ring = ring_of(owners)
    table = np.zeros((owners, owners), np.int32)
    for at, here in enumerate(ring):
        for side in (0, 1):
            for turn in range(len(ring)):
                source = 2 * ring[at - turn]
                table[2 * here + side, 2 * turn : 2 * turn + 2] = (source + side, source + 1 - side)
    return table


def local(
    atom_features,
    distances,
    source_index,
    slot_index,
    live_mask,
    output_cot,
    energy_cot,
    attention_weight,
    attention_first,
    attention_second,
    output_weight,
    output_first,
    output_second,
    gateup_weight,
    gateup_first,
    gateup_second,
    down_weight,
    down_first,
    down_second,
    basis_weight,
    basis_first,
    basis_second,
    readout_weight,
    readout_first,
    readout_second,
    norm_gains,
    gains_first,
    gains_second,
):
    features = atom_features[0]
    atoms = features.shape[0]
    slots = slot_index.shape[2]
    edges = atoms * slots
    owners = H // output_weight.shape[1]
    sent = edges // owners
    wa, wo, wg, wd, wb, wr = (
        attention_weight.shape[1],
        output_weight.shape[1],
        gateup_weight.shape[1],
        down_weight.shape[1],
        basis_weight.shape[1],
        readout_weight.shape[0],
    )

    dist = distances[0]
    high = lax.reduce_precision(dist, 8, 7)
    middle = lax.reduce_precision(dist - high, 8, 7)
    lower = dist - high - middle
    source = source_index[0]
    pieces = (high, middle, lower, source >> 5, source & 31)
    meta = jnp.stack([piece.astype(BF16) for piece in pieces])
    meta = meta.reshape(5, owners, sent // H, H).transpose(1, 0, 2, 3)
    meta_rows = 5 * sent // H
    thin = jnp.concatenate([norm_gains, readout_weight[None]], axis=0).astype(BF16).reshape(1, 1, -1)
    thin = jnp.broadcast_to(
        jnp.pad(thin, ((0, 0), (0, 7), (0, H - thin.shape[2]))), (owners, 8, H)
    )
    basis_rows = jnp.pad(basis_weight.T.astype(BF16), ((0, 0), (0, NB_ROWS - NB)))
    weight_rows = jnp.concatenate(
        [
            attention_weight.T.astype(BF16),
            basis_rows.reshape(3 * wb, H),
            gateup_weight.T.astype(BF16),
            down_weight.T.astype(BF16).reshape(wd * (FF // H), H),
            output_weight.T.astype(BF16),
        ],
        axis=0,
    )
    short = -weight_rows.shape[0] % (8 * lax.axis_size("rep"))
    weight_rows = jnp.pad(weight_rows, ((0, short), (0, 0)))

    reps = lax.axis_size("rep")
    share = weight_rows.shape[0] // reps
    share = lax.dynamic_slice_in_dim(weight_rows, lax.axis_index("rep") * share, share, 0)
    share = jnp.broadcast_to(share[None], (owners, *share.shape))
    meta = jnp.concatenate([meta.reshape(owners, meta_rows, H), thin, share], axis=1)
    meta = lax.all_to_all(meta, "edge", 0, 0, tiled=True)
    share = meta[:, meta_rows + 8 :]
    small = meta[:, meta_rows, : 3 * wr].reshape(owners, 3, wr)
    small = small.transpose(1, 0, 2).reshape(3, H)
    small = jnp.pad(small.astype(F32), ((0, 5), (0, 0)))
    pieces = meta[:, :meta_rows].reshape(owners, 5, sent).astype(F32)
    dist = pieces[:, 0] + pieces[:, 1] + pieces[:, 2]
    source = pieces[:, 3] * 32.0 + pieces[:, 4]

    size = min(GROUP, sent)
    dist_cols, src_cols = (
        values.reshape(owners, sent // size, size // LANES, LANES).transpose(0, 1, 3, 2)
        for values in (dist, source)
    )
    src_rows = source[:, None]

    table = arrival_order(owners)
    me = lax.axis_index("edge")
    order = jnp.asarray(table)[me]
    place = jnp.asarray(np.argsort(table, axis=1).astype(np.int32))[me]
    turns = owners // 2
    kept, shares = (), first_exchange(share)
    pair = (features, pair_swap(features))
    for turn in range(turns):
        coming = None
        if turn < turns - 1:
            ahead = ring_step(pair[0])
            *pair, ahead, order, kept = lax.optimization_barrier((*pair, ahead, order, kept))
            coming = (ahead, pair_swap(ahead))
        kept = (run_edges_forward(2 * turn, order, pair, small, dist_cols, src_cols, kept),)
        if turn == 1:
            *kept, shares = lax.optimization_barrier((*kept, shares))
            weight_rows = share_rows(shares)
        pair = coming
    (kept,) = kept

    at = 0
    fulls = []
    for width, rows in ((H, wa), (NB_ROWS, wb), (H, wg), (FF, wd), (H, wo)):
        count = rows * width // H
        fulls.append(weight_rows[:, at : at + count].reshape(owners * rows, width))
        at += count
    attention_rows, basis_rows, gateup_rows, down_rows, output_rows = fulls
    query_rows, kv_rows = attention_rows[:H], attention_rows[H:]
    wide = jnp.concatenate([kv_rows, basis_rows[:, :NB_PAD]], axis=1)

    slot_ids = slot_index[0]
    slot_owner = slot_ids // sent
    arrived = sum(jnp.where(slot_owner == s, place[s], 0) for s in range(owners))
    arrived = arrived * sent + slot_ids % sent
    idx = arrived.reshape(atoms // BLOCK, BLOCK, slots).transpose(0, 2, 1).reshape(-1) * 4
    count = jnp.sum(live_mask[0], axis=1, keepdims=True).astype(F32)
    core = (lax.axis_index("rep") & 1).astype(jnp.int32)[None]
    block_out, energy, d_after, d_normed_own, d_rows, grads_mine, grads_theirs = run_atoms(
        owners,
        idx,
        core,
        kept,
        features,
        output_cot[0],
        energy_cot[0][:, None],
        count,
        small,
        wide,
        query_rows,
        output_rows,
        gateup_rows,
        down_rows,
    )
    turns_back = [*range(1, turns), 0]
    bits = halves(lax.axis_size("rep"))[1:]
    fetched = across(grads_theirs, 0)
    parts, after, running = [], (), None

    def add_pair(number, latest):
        part, other = parts[number]
        if running is None:
            return part.astype(F32) + behind(other, latest).astype(F32)
        moved = behind(ring_step(running), latest)
        return part.astype(F32) + other.astype(F32) + moved.astype(F32)

    for number, turn in enumerate(turns_back):
        part, part_other = run_edges_backward(turn, order, d_rows, src_rows, atoms, after)
        parts.append((part, pair_swap(part_other)))
        after = ()
        if number == 1:
            totals = grads_mine.astype(F32) + behind(fetched, part).astype(F32)
            totals, sent_rows = halve(totals.reshape(owners, -1, LANES), bits[0])
            fetched = across(sent_rows, bits[0])
            after = (sent_rows,)
        elif 1 < number < turns - 1:
            running = add_pair(number - 2, part).astype(BF16)
            after = (running,)
    totals = totals + behind(fetched, part).astype(F32)
    for bit in bits[1:]:
        totals, sent_rows = halve(totals, bit)
        totals = totals + across(sent_rows, bit).astype(F32)
    side = me & 1
    totals = totals.reshape(turns, 2, *totals.shape[1:])
    sent_rows = lax.dynamic_index_in_dim(totals, 1 - side, 1, keepdims=False).astype(BF16)
    totals = lax.dynamic_index_in_dim(totals, side, 1, keepdims=False)
    fetched = pair_swap(sent_rows)
    latest, held = sent_rows, None
    for number in range(turns - 3, turns):
        total = add_pair(number, latest)
        running = total.astype(BF16)
        if number == turns - 3:
            totals = totals + behind(fetched, running).astype(F32)
            held = ring_rows(totals, order, turns_back[:1], None)
        elif number == turns - 2:
            held = ring_rows(totals, order, turns_back[1:-1], behind(held, running))
        latest = held
    held = ring_rows(totals, order, turns_back[-1:], held)
    d_from_edges = total
    held, fetched = gather_back(held)

    features = features.astype(F32)
    inv_one = inverse_rms(features)
    d_normed_one = d_normed_own + d_from_edges
    scaled = d_normed_one * small[0:1]
    input_grad = (
        d_after
        + inv_one * scaled
        - features * inv_one**3 * jnp.mean(scaled * features, axis=-1, keepdims=True)
    )

    where = jnp.stack([core[0], me.astype(jnp.int32)])
    states = (
        (attention_weight, attention_first, attention_second),
        (output_weight, output_first, output_second),
        (gateup_weight, gateup_first, gateup_second),
        (down_weight, down_first, down_second),
        (basis_weight, basis_first, basis_second),
        (readout_weight, readout_first, readout_second),
        (norm_gains, gains_first, gains_second),
    )

    def turn_over(number, array):
        return array.T if number in (0, 1, 3, 4) else array[None] if number == 5 else array

    updated = run_adamw(
        where,
        held,
        fetched,
        [[turn_over(number, array) for array in triple] for number, triple in enumerate(states)],
    )
    flat = [
        array[0] if at // 3 == 5 else turn_over(at // 3, array)
        for at, array in enumerate(updated[:21])
    ]
    lows = [turn_over(number, array) for number, array in enumerate(updated[21:])]
    return (block_out[None], energy[:, 0][None], input_grad[None], *flat, *lows)


def solution(mesh):
    matrix = P(None, "edge")
    rows = P("rep", "edge", None)
    pairs = P("rep", "edge")
    weights = (matrix,) * 15 + (P("edge"),) * 3 + (matrix,) * 3
    return jax.shard_map(
        local,
        mesh=mesh,
        in_specs=(rows, pairs, pairs, rows, rows, rows, pairs) + weights,
        out_specs=(rows, pairs, rows) + weights + (matrix,) * 5,
        check_vma=False,
    )
```

```python
import functools
import math

import jax
import jax.numpy as jnp
import numpy as np
from jax import lax
from jax.experimental import pallas as pl
from jax.experimental.pallas import tpu as pltpu
from jax.sharding import PartitionSpec as P

H = 256
HEADS = 8
FF = 1024
NB = 600
STEP = 5
HEAD_DIM = 32

EPS = 1e-06
CUTOFF = 6.0
BETA_ONE = 0.5
BETA_TWO = 0.5
ADAM_EPS = 1e-08
DECAY = 0.01

LANES = 128
NB_PAD = 640
NB_ROWS = 768
WIDE = H + NB_PAD
CHUNK = 1024
BLOCK = 128
GROUP = 1024
UNROLL = 16
VMEM_BYTES = 60 * 1024 * 1024

F32 = jnp.float32
BF16 = jnp.bfloat16


def dot_nn(left, right):
    return jnp.dot(left, right, preferred_element_type=F32)


def dot_nt(left, right):
    return lax.dot_general(left, right, (((1,), (1,)), ((), ())), preferred_element_type=F32)


def dot_tn(left, right):
    return lax.dot_general(left, right, (((0,), (0,)), ((), ())), preferred_element_type=F32)


def inverse_rms(rows):
    return lax.rsqrt(jnp.mean(rows * rows, axis=-1, keepdims=True) + EPS)


def edges_forward(count, order_ref, small_ref, dist_ref, src_ref, *rest):
    feature_refs, (kept_ref, normed_ref) = rest[:count], rest[-2:]
    atoms = normed_ref.shape[0]

    def norm(ref):
        features = ref[...].astype(F32)
        normed_ref[...] = (features * inverse_rms(features) * small_ref[0:1, :]).astype(BF16)

    first = pl.program_id(1) == 0
    for number, ref in enumerate(feature_refs):
        pl.when(jnp.logical_and(first, pl.program_id(0) == number))(functools.partial(norm, ref))
    atom_lane = lax.broadcasted_iota(jnp.int32, (1, atoms), 1).astype(F32)
    centres = lax.broadcasted_iota(jnp.int32, (1, NB_PAD), 1).astype(F32) * (CUTOFF / (NB - 1))
    per_spread = math.sqrt(math.log2(math.e)) / (2.0 * CUTOFF / (NB - 1))
    picks, bases = [], []
    for column in range(dist_ref.shape[3]):
        source = src_ref[0, 0, :, column : column + 1]
        picks.append(jnp.where(source == atom_lane, 1.0, 0.0).astype(BF16))
        offset = (dist_ref[0, 0, :, column : column + 1] - centres) * per_spread
        bases.append(jnp.exp2(-(offset * offset)).astype(BF16))
    kept_ref[:, :H] = dot_nn(jnp.concatenate(picks, axis=0), normed_ref[...]).astype(BF16)
    kept_ref[:, H:] = jnp.concatenate(bases, axis=0)


def atoms_kernel(
    ins, blocks, outs, owners,
    idx_ref, core_ref, kept_ref, x_ref, cot_ref, ecot_ref, count_ref, small_ref,
    wide_ref, query_ref, output_ref, gateup_ref, down_ref,
    block_ref, energy_ref, after_ref, dnorm_ref, drows_ref, mine_ref, theirs_ref,
    rows, stage, products, spread_out, sum_up,
    gwide_ref, ggateup_ref, gdown_ref, goutput_ref, gquery_ref, gsmall_ref,
):
    step = pl.program_id(0)
    scaling = HEAD_DIM ** (-0.5)
    slots = stage.shape[0] // (4 * BLOCK)
    pairs = slots * HEADS

    @pl.when(step == 0)
    def _():
        for ref in (gwide_ref, ggateup_ref, gdown_ref, goutput_ref, gquery_ref, gsmall_ref):
            ref[...] = jnp.zeros_like(ref)
        lane = lax.broadcasted_iota(jnp.int32, (pairs, slots * H), 1) // HEAD_DIM
        pair = lax.broadcasted_iota(jnp.int32, (pairs, slots * H), 0)
        spread_out[...] = jnp.where(lane == pair, 1.0, 0.0).astype(BF16)
        lane = lax.broadcasted_iota(jnp.int32, (slots * H, pairs), 0) // HEAD_DIM
        pair = lax.broadcasted_iota(jnp.int32, (slots * H, pairs), 1)
        sum_up[...] = jnp.where(lane == pair, 1.0, 0.0).astype(BF16)

    @pl.when(step < ins)
    def _():
        base = pl.multiple_of(step * (CHUNK * 4), CHUNK * 4)
        edge_kv = dot_nt(kept_ref[...], wide_ref[...]).astype(BF16).astype(F32)
        for part in range(4):
            rows[pl.ds(base + part, CHUNK, stride=4), :] = edge_kv[
                :, part * LANES : (part + 1) * LANES
            ]

    @pl.when(jnp.logical_and(step >= ins, step < ins + blocks))
    def _():
        block = step - ins
        total = slots * BLOCK
        base = block * total

        def fetch(turn, carry):
            for inner in range(UNROLL):
                row = turn * UNROLL + inner
                at = pl.multiple_of(idx_ref[base + row], 4)
                stage[pl.ds(pl.multiple_of(row * 4, 4), 4), :] = rows[pl.ds(at, 4), :]
            return carry

        lax.fori_loop(0, total // UNROLL, fetch, 0)

        def staged(slot, part):
            first = slot * (4 * BLOCK) + 2 * part
            return jnp.concatenate(
                [stage[pl.ds(first + half, BLOCK, stride=4), :] for half in (0, 1)], axis=1
            )

        def put(slot, part, value):
            first = slot * (4 * BLOCK) + 2 * part
            for half in (0, 1):
                stage[pl.ds(first + half, BLOCK, stride=4), :] = value[
                    :, half * LANES : (half + 1) * LANES
                ]

        def over_slots(values, combine):
            shift = HEADS
            while shift < pairs:
                values = combine(values, pltpu.roll(values, shift, 1))
                shift *= 2
            return values

        def over_features(left, part):
            for slot in range(slots):
                products[:, slot * H : (slot + 1) * H] = (left * staged(slot, part)).astype(BF16)
            return dot_nn(products[...], sum_up[...])

        gain_one = small_ref[0:1, :]
        gain_two = small_ref[1:2, :]
        reader = small_ref[2:3, :]
        features = x_ref[...].astype(F32)
        inv_one = inverse_rms(features)
        normed_one = (features * inv_one * gain_one).astype(BF16)
        queries = dot_nt(normed_one, query_ref[...]).astype(BF16).astype(F32)

        scores = over_features(queries, 0) * scaling
        slot_of = lax.broadcasted_iota(jnp.int32, (1, pairs), 1) // HEADS
        scores = jnp.where(slot_of.astype(F32) < count_ref[...], scores, -1e30)
        terms = jnp.exp(scores - over_slots(scores, jnp.maximum))
        soft = terms / over_slots(terms, jnp.add)
        soft_low = soft.astype(BF16)

        def spread(values, slot):
            return dot_nn(values, spread_out[:, slot * H : (slot + 1) * H])

        mixture = jnp.zeros((BLOCK, H), F32)
        for slot in range(slots):
            mixture += spread(soft_low, slot) * staged(slot, 1)
        mixture = mixture.astype(BF16)

        after = features + dot_nt(mixture, output_ref[...])
        inv_two = inverse_rms(after)
        normed_two = (after * inv_two * gain_two).astype(BF16)
        gate_up = dot_nt(normed_two, gateup_ref[...])
        ff = gate_up.shape[1] // 2
        gate, up_part = gate_up[:, :ff], gate_up[:, ff:]
        gate_sig = 1.0 / (1.0 + jnp.exp(-gate))
        swished = gate * gate_sig
        hidden = (swished * up_part).astype(BF16)
        result = after + dot_nt(hidden, down_ref[...])
        block_ref[...] = result.astype(BF16)
        energy_ref[...] = jnp.broadcast_to(
            jnp.sum(result * reader, axis=-1, keepdims=True), energy_ref.shape
        )
        energy_row = ecot_ref[...]
        d_result = cot_ref[...].astype(F32) + energy_row * reader
        grad_read = jnp.sum(energy_row * result, axis=0, keepdims=True)
        d_ffn = d_result.astype(BF16)
        gdown_ref[...] += dot_tn(d_ffn, hidden)
        d_hidden = dot_nn(d_ffn, down_ref[...])
        d_gate = d_hidden * up_part * gate_sig * (1.0 + gate * (1.0 - gate_sig))
        d_gate_up = jnp.concatenate(
            [d_gate.astype(BF16), (d_hidden * swished).astype(BF16)], axis=1
        )
        ggateup_ref[...] += dot_tn(d_gate_up, normed_two)
        d_normed_two = dot_nn(d_gate_up, gateup_ref[...])
        scaled = d_normed_two * gain_two
        grad_gain_two = jnp.sum(d_normed_two * after * inv_two, axis=0, keepdims=True)
        d_after = (
            d_result
            + inv_two * scaled
            - after * (inv_two * inv_two * inv_two)
            * jnp.mean(scaled * after, axis=-1, keepdims=True)
        )
        after_ref[...] = d_after
        d_attn = d_after.astype(BF16)
        goutput_ref[...] += dot_tn(d_attn, mixture)
        d_mixture = dot_nn(d_attn, output_ref[...]).astype(BF16).astype(F32)

        d_soft = over_features(d_mixture, 1)
        d_scores = soft * (d_soft - over_slots(soft * d_soft, jnp.add))
        d_scores = d_scores.astype(BF16)
        scaled_queries = queries * scaling
        d_queries = jnp.zeros((BLOCK, H), F32)
        for slot in range(slots):
            wide_scores = spread(d_scores, slot)
            d_queries += wide_scores * staged(slot, 0)
            put(slot, 0, wide_scores * scaled_queries)
            put(slot, 1, spread(soft_low, slot) * d_mixture)
        d_queries = (d_queries * scaling).astype(BF16)
        gquery_ref[...] += dot_tn(d_queries, normed_one)
        d_normed = dot_nn(d_queries, query_ref[...])
        dnorm_ref[...] = d_normed
        grad_gain_one = jnp.sum(d_normed * features * inv_one, axis=0, keepdims=True)
        gsmall_ref[0:1, :] += grad_gain_one
        gsmall_ref[1:2, :] += grad_gain_two
        gsmall_ref[2:3, :] += grad_read

        def spill(turn, carry):
            for inner in range(UNROLL):
                row = turn * UNROLL + inner
                at = pl.multiple_of(idx_ref[base + row], 4)
                rows[pl.ds(at, 4), :] = stage[pl.ds(pl.multiple_of(row * 4, 4), 4), :]
            return carry

        lax.fori_loop(0, total // UNROLL, spill, 0)

    @pl.when(step >= ins + blocks)
    def _():
        base = pl.multiple_of((step - ins - blocks) * (CHUNK * 4), CHUNK * 4)
        d_edges = jnp.concatenate(
            [rows[pl.ds(base + part, CHUNK, stride=4), :].astype(BF16) for part in range(4)], axis=1
        )
        gwide_ref[...] += dot_tn(d_edges, kept_ref[...])
        drows_ref[...] = dot_nn(d_edges, wide_ref[:, :H]).astype(BF16)

    @pl.when(step == ins + blocks + outs - 1)
    def _():
        shares = gwide_ref[:, :H] * wide_ref[:, :H].astype(F32)
        gsmall_ref[0:1, :] += jnp.sum(shares, axis=0, keepdims=True) / small_ref[0:1, :]
        size = mine_ref.shape[0]
        height = size // owners
        for owner in range(owners):
            for half in (0, 1):
                at = half * size + owner * height
                for ref, first, count, columns in packed_pieces(
                    owner, owners, gquery_ref, gwide_ref, ggateup_ref, gdown_ref, goutput_ref
                ):
                    for low in range(columns.start + half * LANES, columns.stop, H):
                        if low < ref.shape[1]:
                            rows[at : at + count, :] = ref[
                                first : first + count, low : low + LANES
                            ]
                        at += count
                rows[at : at + 8, :] = gsmall_ref[:, half * LANES : (half + 1) * LANES]
        core = core_ref[0]
        for ref, half in ((mine_ref, core), (theirs_ref, 1 - core)):
            ref[...] = rows[pl.ds(pl.multiple_of(half * size, 8), size), :].astype(BF16)


def packed_pieces(owner, owners, query, wide, gateup, down, output):
    count = 3 * H // owners
    first, last = owner * count, (owner + 1) * count
    if first < H:
        yield query, first, min(last, H) - first, range(H)
    if last > H:
        yield wide, max(first, H) - H, last - max(first, H), range(H)
    share = 2 * H // owners
    yield wide, owner * share, share, range(H, H + NB_ROWS)
    for ref in (gateup, down, output):
        share = ref.shape[0] // owners
        yield ref, owner * share, share, range(ref.shape[1])


def edges_backward(order_ref, rows_ref, src_ref, *rest):
    mine_ref, other_ref = rest[-2:]
    d_rows = rows_ref[...]
    source = src_ref[0]
    step = 256

    def sums(ref):
        for start in range(0, ref.shape[0], step):
            atom = lax.broadcasted_iota(jnp.int32, (step, 1), 0).astype(F32) + float(start)
            pick = jnp.where(atom == source, 1.0, 0.0).astype(BF16)
            ref[start : start + step, :] = dot_nn(pick, d_rows).astype(ref.dtype)

    pl.when(pl.program_id(0) == 0)(lambda: sums(mine_ref))
    pl.when(pl.program_id(0) == 1)(lambda: sums(other_ref))


def adamw_step(weight, first_mom, second, gradient, step_rate):
    first_new = BETA_ONE * first_mom + (1.0 - BETA_ONE) * gradient
    second_new = BETA_TWO * second + (1.0 - BETA_TWO) * gradient * gradient
    fix_one = 1.0 - BETA_ONE**STEP
    fix_two = 1.0 - BETA_TWO**STEP
    direction = first_new / fix_one / (jnp.sqrt(second_new / fix_two) + ADAM_EPS) + DECAY * weight
    return (first_new, second_new, weight - step_rate * direction)


def adamw_kernel(where_ref, held_ref, fetched_ref, *refs):
    ins, outs, lows = refs[:21], refs[21:42], refs[42:47]
    left, right = refs[47:]
    core = where_ref[0]
    for here in (0, 1):

        @pl.when(core == here)
        def _():
            for ref, half in ((held_ref, here), (fetched_ref, 1 - here)):
                (left, right)[half][...] = ref[...]

    def packed(at, rows, pieces=1):
        halves = [
            half[at + part * rows : at + (part + 1) * rows, :]
            for part in range(pieces)
            for half in (left, right)
        ]
        return jnp.concatenate(halves, axis=1)

    wa, wo, wd, wb = (ins[3 * number].shape[0] for number in (0, 1, 3, 4))
    wg = ins[6].shape[1]
    at = 0
    attention = packed(at, wa)
    at += wa
    basis = packed(at, wb, NB_ROWS // H)[:, :NB]
    at += wb * (NB_ROWS // H)
    gateup = packed(at, wg)
    if wg < LANES:
        gateup = jnp.concatenate([gateup, jnp.zeros((LANES - wg, H), F32)], axis=0)
    gateup = gateup.T[:, :wg]
    at += wg
    down = packed(at, wd, FF // H)
    at += wd * (FF // H)
    output = packed(at, wo)
    at += wo
    thin = packed(at, 8)
    width = ins[15].shape[1]
    column = lax.broadcasted_iota(jnp.int32, (H, width), 0)
    mine = lax.broadcasted_iota(jnp.int32, (H, width), 1) + where_ref[1] * width
    thin = jnp.dot(
        thin,
        jnp.where(column == mine, 1.0, 0.0),
        precision=lax.Precision.HIGHEST,
        preferred_element_type=F32,
    )
    gradients = (attention, output, gateup, down, basis, thin[2:3], thin[:2])
    rates = (H ** (-0.5), (H // 16) ** (-0.5), H ** (-0.5), FF ** (-0.5), 0.5, H ** (-0.5), 0.2)
    for number, (gradient, rate) in enumerate(zip(gradients, rates, strict=True)):
        weight, first, second = (ref[...] for ref in ins[3 * number : 3 * number + 3])
        results = adamw_step(weight, first, second, gradient, rate)
        for ref, value in zip(outs[3 * number : 3 * number + 3], results, strict=True):
            ref[...] = value
        if number < 5:
            lows[number][...] = results[2].astype(BF16)


def run_adamw(where, held, fetched, states):
    arrays = [array for triple in states for array in triple]
    spec = pl.BlockSpec(memory_space=pltpu.VMEM)
    shapes = [
        jax.ShapeDtypeStruct(array.shape, F32) for triple in states for array in (*triple[1:], triple[0])
    ]
    shapes += [jax.ShapeDtypeStruct(triple[0].shape, BF16) for triple in states[:5]]
    return list(
        pl.pallas_call(
            adamw_kernel,
            in_specs=[pl.BlockSpec(memory_space=pltpu.SMEM)] + [spec] * (2 + len(arrays)),
            out_specs=[spec] * len(shapes),
            out_shape=shapes,
            scratch_shapes=[pltpu.VMEM(held.shape, F32)] * 2,
            compiler_params=pltpu.CompilerParams(vmem_limit_bytes=VMEM_BYTES),
        )(where, held, fetched, *arrays)
    )


def whole_spec(shape):
    return pl.BlockSpec(shape, lambda *_: (0,) * len(shape), pipeline_mode=pl.Buffered(1))


def run_edges_forward(place, order, sources, small, dist_cols, src_cols, before):
    atoms = sources[0].shape[0]
    count = len(sources)
    owners, groups, _, columns = dist_cols.shape
    size = columns * LANES

    def picked(i, g, order_ref):
        return (order_ref[place + i], g, 0, 0)

    return pl.pallas_call(
        functools.partial(edges_forward, count),
        grid_spec=pltpu.PrefetchScalarGridSpec(
            num_scalar_prefetch=1,
            grid=(count, groups),
            in_specs=[
                whole_spec(small.shape),
                pl.BlockSpec((1, 1, LANES, columns), picked),
                pl.BlockSpec((1, 1, LANES, columns), picked),
            ]
            + [whole_spec(source.shape) for source in sources]
            + [pl.BlockSpec(memory_space=pl.ANY)] * len(before),
            out_specs=pl.BlockSpec(
                (size, WIDE), lambda i, g, order_ref: ((place + i) * groups + g, 0)
            ),
            scratch_shapes=[pltpu.VMEM((atoms, H), BF16)],
        ),
        out_shape=jax.ShapeDtypeStruct((owners * groups * size, WIDE), BF16),
        input_output_aliases={4 + count: 0} if before else {},
        compiler_params=pltpu.CompilerParams(vmem_limit_bytes=VMEM_BYTES),
        cost_estimate=pl.CostEstimate(
            flops=2 * count * groups * size * atoms * H,
            bytes_accessed=count * (groups * size * 2 * WIDE + atoms * H * 2),
            transcendentals=count * groups * size * NB_PAD,
        ),
    )(order, small, dist_cols, src_cols, *sources, *before)


def run_atoms(
    owners, idx, core, kept, features, cot, ecot, count, small, wide, query, output, gateup, down
):
    edges, atoms = kept.shape[0], features.shape[0]
    ins, blocks = edges // CHUNK, atoms // BLOCK
    outs = ins
    slots = edges // atoms
    ff = down.shape[1]
    height = (3 * H + 3 * 2 * H + gateup.shape[0] + ff // H * H + H) // owners + 8

    def atom_block(i):
        return (jnp.clip(i - ins, 0, blocks - 1), 0)

    def edge_block(i):
        return (jnp.where(i < ins, i, jnp.maximum(i - ins - blocks, 0)), 0)

    return pl.pallas_call(
        functools.partial(atoms_kernel, ins, blocks, outs, owners),
        grid=(ins + blocks + outs,),
        in_specs=[
            pl.BlockSpec(memory_space=pltpu.SMEM),
            pl.BlockSpec(memory_space=pltpu.SMEM),
            pl.BlockSpec((CHUNK, WIDE), edge_block),
            pl.BlockSpec((BLOCK, H), atom_block),
            pl.BlockSpec((BLOCK, H), atom_block),
            pl.BlockSpec((BLOCK, 1), atom_block),
            pl.BlockSpec((BLOCK, 1), atom_block),
            whole_spec(small.shape),
            whole_spec(wide.shape),
            whole_spec(query.shape),
            whole_spec(output.shape),
            whole_spec(gateup.shape),
            whole_spec(down.shape),
        ],
        out_specs=[
            pl.BlockSpec((BLOCK, H), atom_block),
            pl.BlockSpec((BLOCK, LANES), atom_block),
            pl.BlockSpec((BLOCK, H), atom_block),
            pl.BlockSpec((BLOCK, H), atom_block),
            pl.BlockSpec((CHUNK, H), lambda i: (jnp.maximum(i - ins - blocks, 0), 0)),
            whole_spec((owners * height, LANES)),
            whole_spec((owners * height, LANES)),
        ],
        out_shape=[
            jax.ShapeDtypeStruct((atoms, H), BF16),
            jax.ShapeDtypeStruct((atoms, LANES), F32),
            jax.ShapeDtypeStruct((atoms, H), F32),
            jax.ShapeDtypeStruct((atoms, H), F32),
            jax.ShapeDtypeStruct((edges, H), BF16),
            jax.ShapeDtypeStruct((owners * height, LANES), BF16),
            jax.ShapeDtypeStruct((owners * height, LANES), BF16),
        ],
        scratch_shapes=[
            pltpu.VMEM((edges * 4 + 8, LANES), F32),
            pltpu.VMEM((slots * BLOCK * 4 + 8, LANES), F32),
            pltpu.VMEM((BLOCK, slots * H), BF16),
            pltpu.VMEM((slots * HEADS, slots * H), BF16),
            pltpu.VMEM((slots * H, slots * HEADS), BF16),
            pltpu.VMEM(wide.shape, F32),
            pltpu.VMEM(gateup.shape, F32),
            pltpu.VMEM(down.shape, F32),
            pltpu.VMEM(output.shape, F32),
            pltpu.VMEM(query.shape, F32),
            pltpu.VMEM((8, H), F32),
        ],
        compiler_params=pltpu.CompilerParams(vmem_limit_bytes=VMEM_BYTES),
        cost_estimate=pl.CostEstimate(
            flops=2 * edges * H * (WIDE * 4 + H * 8) + 2 * atoms * H * ff * 9,
            bytes_accessed=edges * WIDE * 4 + edges * H * 2 + ff * H * 3 * 6,
            transcendentals=edges * HEADS,
        ),
    )(idx, core, kept, features, cot, ecot, count, small, wide, query, output, gateup, down)


def run_edges_backward(turn, order, d_rows, src_rows, atoms, after):
    owners, sent = src_rows.shape[0], src_rows.shape[2]
    return pl.pallas_call(
        edges_backward,
        grid_spec=pltpu.PrefetchScalarGridSpec(
            num_scalar_prefetch=1,
            grid=(2,),
            in_specs=[
                pl.BlockSpec((sent, H), lambda i, order_ref: (2 * turn + i, 0)),
                pl.BlockSpec((1, 1, sent), lambda i, order_ref: (order_ref[2 * turn + i], 0, 0)),
            ]
            + [pl.BlockSpec(memory_space=pl.ANY)] * len(after),
            out_specs=[whole_spec((atoms, H)), whole_spec((atoms, H))],
        ),
        out_shape=[jax.ShapeDtypeStruct((atoms, H), BF16)] * 2,
        compiler_params=pltpu.CompilerParams(vmem_limit_bytes=VMEM_BYTES),
        cost_estimate=pl.CostEstimate(
            flops=4 * sent * atoms * H,
            bytes_accessed=2 * sent * 2 * H + 4 * atoms * H,
            transcendentals=0,
        ),
    )(order, d_rows, src_rows, *after)


def halves(axis_size):
    return range((axis_size - 1).bit_length())


def across(array, bit):
    size = lax.axis_size("rep")
    return lax.ppermute(array, "rep", [(r, r ^ (1 << bit)) for r in range(size)])


def first_exchange(held):
    bit = halves(lax.axis_size("rep"))[-1]
    return {0: held, 1 << bit: across(held, bit)}


def share_rows(shares):
    reps = lax.axis_size("rep")
    me = lax.axis_index("rep")
    held = shares[0]
    for bit in reversed(halves(reps)[:-1]):
        shares = shares | {
            number | (1 << bit): across(array, bit) for number, array in shares.items()
        }
    ordered = []
    for batch in range(reps):
        share = held
        for number in range(1, reps):
            share = jnp.where(me ^ batch == number, shares[number], share)
        ordered.append(share)
    return jnp.concatenate(ordered, axis=1)


def behind(array, other):
    return lax.optimization_barrier((array, other))[0]


def halve(totals, bit):
    half = totals.shape[1] // 2
    upper = (lax.axis_index("rep") >> bit) & 1
    sent = lax.dynamic_slice_in_dim(totals, (1 - upper) * half, half, 1)
    return lax.dynamic_slice_in_dim(totals, upper * half, half, 1), sent.astype(BF16)


def ring_rows(totals, order, turns, running):
    for turn in turns:
        total = lax.dynamic_index_in_dim(totals, order[2 * turn] >> 1, 0, keepdims=False)
        if running is not None:
            total = total + ring_step(running.astype(BF16)).astype(F32)
        running = total
    return running


def gather_back(held):
    reps = lax.axis_size("rep")
    me = lax.axis_index("rep")
    for bit in reversed(halves(reps)[1:]):
        fetched = across(held, bit)
        upper = (me >> bit) & 1 == 1
        held = jnp.concatenate(
            [jnp.where(upper, fetched, held), jnp.where(upper, held, fetched)], axis=0
        )
    return held, across(held, 0)


def ring_of(owners):
    pairs = owners // 2
    return [*range(0, pairs, 2), *reversed(range(1, pairs, 2))]


def ring_step(array):
    owners = lax.axis_size("edge")
    ring = ring_of(owners)
    moves = [
        (2 * here + side, 2 * ring[(at + 1) % len(ring)] + side)
        for at, here in enumerate(ring)
        for side in (0, 1)
    ]
    return lax.ppermute(array, "edge", moves)


def pair_swap(array):
    owners = lax.axis_size("edge")
    return lax.ppermute(array, "edge", [(e, e ^ 1) for e in range(owners)])


def arrival_order(owners):
    ring = ring_of(owners)
    table = np.zeros((owners, owners), np.int32)
    for at, here in enumerate(ring):
        for side in (0, 1):
            for turn in range(len(ring)):
                source = 2 * ring[at - turn]
                table[2 * here + side, 2 * turn : 2 * turn + 2] = (source + side, source + 1 - side)
    return table


def local(
    atom_features,
    distances,
    source_index,
    slot_index,
    live_mask,
    output_cot,
    energy_cot,
    attention_weight,
    attention_first,
    attention_second,
    output_weight,
    output_first,
    output_second,
    gateup_weight,
    gateup_first,
    gateup_second,
    down_weight,
    down_first,
    down_second,
    basis_weight,
    basis_first,
    basis_second,
    readout_weight,
    readout_first,
    readout_second,
    norm_gains,
    gains_first,
    gains_second,
):
    features = atom_features[0]
    atoms = features.shape[0]
    slots = slot_index.shape[2]
    edges = atoms * slots
    owners = H // output_weight.shape[1]
    sent = edges // owners
    wa, wo, wg, wd, wb, wr = (
        attention_weight.shape[1],
        output_weight.shape[1],
        gateup_weight.shape[1],
        down_weight.shape[1],
        basis_weight.shape[1],
        readout_weight.shape[0],
    )

    table = arrival_order(owners)
    me = lax.axis_index("edge")
    order = jnp.asarray(table)[me]
    place = jnp.asarray(np.argsort(table, axis=1).astype(np.int32))[me]
    turns = owners // 2
    slot_ids = slot_index[0]
    slot_owner = slot_ids // sent
    arrived = sum(jnp.where(slot_owner == s, place[s], 0) for s in range(owners))
    arrived = arrived * sent + slot_ids % sent
    idx = arrived.reshape(atoms // BLOCK, BLOCK, slots).transpose(0, 2, 1).reshape(-1) * 4
    live_count = jnp.sum(live_mask[0], axis=1, keepdims=True).astype(F32)
    energy_rows = energy_cot[0][:, None]
    pair = (features, pair_swap(features))
    ahead = ring_step(features)

    dist = distances[0]
    high = lax.reduce_precision(dist, 8, 7)
    middle = lax.reduce_precision(dist - high, 8, 7)
    lower = dist - high - middle
    source = source_index[0]
    pieces = (high, middle, lower, source >> 5, source & 31)
    meta = jnp.stack([piece.astype(BF16) for piece in pieces])
    meta = meta.reshape(5, owners, sent // H, H).transpose(1, 0, 2, 3)
    meta_rows = 5 * sent // H
    thin = jnp.concatenate([norm_gains, readout_weight[None]], axis=0).astype(BF16).reshape(1, 1, -1)
    thin = jnp.broadcast_to(
        jnp.pad(thin, ((0, 0), (0, 7), (0, H - thin.shape[2]))), (owners, 8, H)
    )
    basis_rows = jnp.pad(basis_weight.T.astype(BF16), ((0, 0), (0, NB_ROWS - NB)))
    weight_rows = jnp.concatenate(
        [
            attention_weight.T.astype(BF16),
            basis_rows.reshape(3 * wb, H),
            gateup_weight.T.astype(BF16),
            down_weight.T.astype(BF16).reshape(wd * (FF // H), H),
            output_weight.T.astype(BF16),
        ],
        axis=0,
    )
    short = -weight_rows.shape[0] % (8 * lax.axis_size("rep"))
    weight_rows = jnp.pad(weight_rows, ((0, short), (0, 0)))

    reps = lax.axis_size("rep")
    share = weight_rows.shape[0] // reps
    share = lax.dynamic_slice_in_dim(weight_rows, lax.axis_index("rep") * share, share, 0)
    share = jnp.broadcast_to(share[None], (owners, *share.shape))
    meta = jnp.concatenate([meta.reshape(owners, meta_rows, H), thin, share], axis=1)
    meta, *pair, ahead = lax.optimization_barrier((meta, *pair, ahead))
    meta = lax.all_to_all(meta, "edge", 0, 0, tiled=True)
    share = meta[:, meta_rows + 8 :]
    small = meta[:, meta_rows, : 3 * wr].reshape(owners, 3, wr)
    small = small.transpose(1, 0, 2).reshape(3, H)
    small = jnp.pad(small.astype(F32), ((0, 5), (0, 0)))
    pieces = meta[:, :meta_rows].reshape(owners, 5, sent).astype(F32)
    dist = pieces[:, 0] + pieces[:, 1] + pieces[:, 2]
    source = pieces[:, 3] * 32.0 + pieces[:, 4]

    size = min(GROUP, sent)
    dist_cols, src_cols = (
        values.reshape(owners, sent // size, size // LANES, LANES).transpose(0, 1, 3, 2)
        for values in (dist, source)
    )
    src_rows = source[:, None]

    kept, shares = (), first_exchange(share)
    order, idx, live_count, energy_rows = lax.optimization_barrier(
        (order, idx, live_count, energy_rows)
    )
    for turn in range(turns):
        coming = None
        if turn < turns - 1:
            if turn > 0:
                ahead = ring_step(pair[0])
            *pair, ahead, order, kept = lax.optimization_barrier((*pair, ahead, order, kept))
            coming = (ahead, pair_swap(ahead))
        kept = (run_edges_forward(2 * turn, order, pair, small, dist_cols, src_cols, kept),)
        if turn == 1:
            *kept, shares = lax.optimization_barrier((*kept, shares))
            weight_rows = share_rows(shares)
        pair = coming
    (kept,) = kept

    at = 0
    fulls = []
    for width, rows in ((H, wa), (NB_ROWS, wb), (H, wg), (FF, wd), (H, wo)):
        count = rows * width // H
        fulls.append(weight_rows[:, at : at + count].reshape(owners * rows, width))
        at += count
    attention_rows, basis_rows, gateup_rows, down_rows, output_rows = fulls
    query_rows, kv_rows = attention_rows[:H], attention_rows[H:]
    wide = jnp.concatenate([kv_rows, basis_rows[:, :NB_PAD]], axis=1)

    core = (lax.axis_index("rep") & 1).astype(jnp.int32)[None]
    block_out, energy, d_after, d_normed_own, d_rows, grads_mine, grads_theirs = run_atoms(
        owners,
        idx,
        core,
        kept,
        features,
        output_cot[0],
        energy_rows,
        live_count,
        small,
        wide,
        query_rows,
        output_rows,
        gateup_rows,
        down_rows,
    )
    turns_back = [*range(1, turns), 0]
    bits = halves(lax.axis_size("rep"))[1:]
    fetched = across(grads_theirs, 0)
    parts, after, running = [], (), None

    def add_pair(number, latest):
        part, other = parts[number]
        if running is None:
            return part.astype(F32) + behind(other, latest).astype(F32)
        moved = behind(ring_step(running), latest)
        return part.astype(F32) + other.astype(F32) + moved.astype(F32)

    for number, turn in enumerate(turns_back):
        part, part_other = run_edges_backward(turn, order, d_rows, src_rows, atoms, after)
        parts.append((part, pair_swap(part_other)))
        after = ()
        if number == 1:
            totals = grads_mine.astype(F32) + behind(fetched, part).astype(F32)
            totals, sent_rows = halve(totals.reshape(owners, -1, LANES), bits[0])
            fetched = across(sent_rows, bits[0])
            after = (sent_rows,)
        elif 1 < number < turns - 1:
            running = add_pair(number - 2, part).astype(BF16)
            after = (running,)
    totals = totals + behind(fetched, part).astype(F32)
    for bit in bits[1:]:
        totals, sent_rows = halve(totals, bit)
        totals = totals + across(sent_rows, bit).astype(F32)
    side = me & 1
    totals = totals.reshape(turns, 2, *totals.shape[1:])
    sent_rows = lax.dynamic_index_in_dim(totals, 1 - side, 1, keepdims=False).astype(BF16)
    totals = lax.dynamic_index_in_dim(totals, side, 1, keepdims=False)
    fetched = pair_swap(sent_rows)
    latest, held = sent_rows, None
    for number in range(turns - 3, turns):
        total = add_pair(number, latest)
        running = total.astype(BF16)
        if number == turns - 3:
            totals = totals + behind(fetched, running).astype(F32)
            held = ring_rows(totals, order, turns_back[:1], None)
        elif number == turns - 2:
            held = ring_rows(totals, order, turns_back[1:-1], behind(held, running))
        latest = held
    held = ring_rows(totals, order, turns_back[-1:], held)
    d_from_edges = total
    held, fetched = gather_back(held)

    features = features.astype(F32)
    inv_one = inverse_rms(features)
    d_normed_one = d_normed_own + d_from_edges
    scaled = d_normed_one * small[0:1]
    input_grad = (
        d_after
        + inv_one * scaled
        - features * inv_one**3 * jnp.mean(scaled * features, axis=-1, keepdims=True)
    )

    where = jnp.stack([core[0], me.astype(jnp.int32)])
    states = (
        (attention_weight, attention_first, attention_second),
        (output_weight, output_first, output_second),
        (gateup_weight, gateup_first, gateup_second),
        (down_weight, down_first, down_second),
        (basis_weight, basis_first, basis_second),
        (readout_weight, readout_first, readout_second),
        (norm_gains, gains_first, gains_second),
    )

    def turn_over(number, array):
        return array.T if number in (0, 1, 3, 4) else array[None] if number == 5 else array

    updated = run_adamw(
        where,
        held,
        fetched,
        [[turn_over(number, array) for array in triple] for number, triple in enumerate(states)],
    )
    flat = [
        array[0] if at // 3 == 5 else turn_over(at // 3, array)
        for at, array in enumerate(updated[:21])
    ]
    lows = [turn_over(number, array) for number, array in enumerate(updated[21:])]
    return (block_out[None], energy[:, 0][None], input_grad[None], *flat, *lows)


def solution(mesh):
    matrix = P(None, "edge")
    rows = P("rep", "edge", None)
    pairs = P("rep", "edge")
    weights = (matrix,) * 15 + (P("edge"),) * 3 + (matrix,) * 3
    return jax.shard_map(
        local,
        mesh=mesh,
        in_specs=(rows, pairs, pairs, rows, rows, rows, pairs) + weights,
        out_specs=(rows, pairs, rows) + weights + (matrix,) * 5,
        check_vma=False,
    )
```
